32 devices in a mesh: dp: 8 (over y, x, core), expert: 4 (over z).
Axes of the slice: x: 2, y: 2, z: 4, core: 2. Of those that a mesh axis runs over, the one named last changes fastest.
Arguments:
- tokens: bfloat16 [4096, 2048], P(('dp', 'expert')), may hold values from -6 to 6
- cotangent: bfloat16 [4096, 2048], P(('dp', 'expert')), may hold values from -6 to 6
- expert_ids: int32 [4096, 8], P(('dp', 'expert')), may hold values from 0 to 127, as said below
- drop_mask: int32 [4096, 8], P(('dp', 'expert')), may hold values 0 or 1
- gate_table: float32 [4096, 8], P(('dp', 'expert')), may hold values from 0.1 to 1
- gate_weight: bfloat16 [2048, 768], P('dp', 'expert'), may hold values from -0.125 to 0.125
- up_weight: bfloat16 [2048, 768], P('dp', 'expert'), may hold values from -0.125 to 0.125
- down_weight: bfloat16 [768, 2048], P('expert', 'dp'), may hold values from -0.21875 to 0.21875
Outputs:
- grad_tokens: bfloat16 [4096, 2048], P(('dp', 'expert'))
- grad_gate: float32 [2048, 768], P('dp', 'expert')
- grad_up: float32 [2048, 768], P('dp', 'expert')
- grad_down: float32 [768, 2048], P('expert', 'dp')
The draws below stay inside these ranges and needn't reach their ends.
Inputs may be any that keep to these rules, and one draw needn't show every extreme that they name: `expert_ids`: each row names 8 different experts.
All inputs are finite; a program needn't handle non-finite values. No bound on the sum of `drop_mask` on one device may be relied on, other than what follows from the above.
Results may differ from the reference program's by a relative error of at most 0.018.
Values may be sent and summed in bfloat16 or wider, within the bound.
No kernel may reach another device: no remote copies, remote signals or barrier semaphores. Data moves between devices by JAX's collectives and lax.ppermute only.
A program may use at most 64 MiB of HBM per device.

```python
import math
import jax
import jax.numpy as jnp
from jax import lax

D = 2048
FF = 768
EXPERTS = 128
TOP = 8
SPLIT = 4
TOK_DEV = 128
CAP = 16
FLIGHT = 1
TOKENS = 4096
GROUPS = 8


def draw_expert_ids(key, part):
    key = jax.random.fold_in(key, 11)
    base_key, roll_key = jax.random.split(key)
    base_score = jax.random.randint(base_key, (TOKENS, EXPERTS), 0, 1 << 20)
    roll = jax.random.randint(roll_key, (TOKENS, EXPERTS), 0, 1000)
    column = jnp.arange(EXPERTS, dtype=jnp.int32)
    chance = jnp.where(column < FLIGHT, 250 // (1 + column), 0)
    forced = (roll < chance[None, :]).astype(jnp.int32)
    score = (base_score + forced * (1 << 21)) * EXPERTS + column[None, :]
    picked_values, picked = lax.top_k(score, TOP)
    return picked.astype(jnp.int32)


def set_ends(values, stream_key, low, top_value):
    longest = values.shape.index(max(values.shape))
    spots = []
    for shift in (0, 1):
        where = [jax.random.randint(jax.random.fold_in(stream_key, axis), (), 0, length) for axis, length in enumerate(values.shape)]
        where[longest] = (where[longest] + shift) % values.shape[longest]
        spots.append(tuple(where))
    return values.at[spots[0]].set(low).at[spots[1]].set(top_value)


def with_spikes(values, own_key, source, target, blocks, factor):
    owner, partner = [(jnp.arange(values.shape[dim]) // (values.shape[dim] // blocks)).reshape([-1 if axis == dim else 1 for axis in range(values.ndim)]) for dim in (source, target)]
    chosen = jax.random.permutation(own_key, blocks)[partner]
    strong = (owner == chosen) | (owner == (partner + blocks // 2) % blocks)
    return jnp.where(strong, factor * values, values)


def shard_levels(key, shape, cuts, least, largest):
    level = 1.0
    for position, blocks in cuts:
        heights = jax.random.uniform(jax.random.fold_in(jax.random.fold_in(key, 6), position), (blocks,), jnp.float32, least / len(cuts), largest / len(cuts))
        level = level * jnp.repeat(jnp.exp(heights), shape[position] // blocks).reshape((-1,) + (1,) * (len(shape) - 1 - position))
    return level


def scatter_about(own_key, shape, spread, most, shards=(), kind=jnp.bfloat16):
    entries = spread * jax.random.normal(own_key, shape, jnp.float32)
    if shards:
        entries = entries * shard_levels(own_key, shape, shards, -0.22, 0.18)
    return jnp.clip(entries, -most, most).astype(kind)


def heavy_noise(rng, shape, deviation, most, cuts, heavy, kind=jnp.bfloat16):
    result = deviation * jax.random.normal(rng, shape, jnp.float32)
    if cuts:
        result = result * shard_levels(rng, shape, cuts, -0.22, 0.18)
    return jnp.clip(with_spikes(result, jax.random.fold_in(rng, 3), *heavy), -most, most).astype(kind)


def setup_inputs(seed: int = 0) -> dict:
    keys = jax.random.split(jax.random.key(seed), 9)
    return {
        "tokens": heavy_noise(keys[0], (TOKENS, D), 1.0, 6.0, ((0, 32),), (0, 1, 32, 2.75)),
        "cotangent": scatter_about(keys[1], (TOKENS, D), 1.0, 6.0, ((0, 32),)),
        "expert_ids": draw_expert_ids(jax.random.fold_in(keys[8], 71), 0),
        "drop_mask": set_ends((jax.random.randint(keys[3], (TOKENS, TOP), 0, 8) < 7).astype(jnp.int32), jax.random.fold_in(keys[3], 1), 0, 1),
        "gate_table": jnp.clip(jnp.exp(math.log(1.0) - 2.3025851 * jax.random.uniform(keys[4], (TOKENS, TOP), jnp.float32) ** shard_levels(keys[4], (TOKENS, TOP), ((0, 32),), -0.2, 0.2)), 0.1, 1.0),
        "gate_weight": scatter_about(keys[5], (D, FLIGHT * FF), D ** -0.5, 0.125, ((0, 8), (1, 4))),
        "up_weight": scatter_about(keys[6], (D, FLIGHT * FF), D ** -0.5, 0.125, ((0, 8), (1, 4))),
        "down_weight": scatter_about(keys[7], (FLIGHT * FF, D), FF ** -0.5, 0.21875, ((0, 4), (1, 8))),
    }


def silu_parts(pre_gate):
    sigmoid_value = jax.nn.sigmoid(pre_gate)
    return pre_gate * sigmoid_value, sigmoid_value * (1.0 + pre_gate * (1.0 - sigmoid_value))


def slot_table(expert_ids, drop_mask, block_rows, in_flight):
    window = jnp.arange(in_flight, dtype=jnp.int32)
    hit_table = ((expert_ids[:, :, None] == window[None, None, :]) & (drop_mask[:, :, None] == 1)).astype(jnp.int32)
    per_token = jnp.sum(hit_table, axis=1)
    blocked = per_token.reshape(-1, block_rows, in_flight)
    earlier = (jnp.cumsum(blocked, axis=1) - blocked).reshape(-1, in_flight)
    slot_rank = jnp.sum(hit_table * earlier[:, None, :], axis=2)
    is_live = (jnp.sum(hit_table, axis=2) > 0) & (slot_rank < CAP)
    return jnp.where(is_live, expert_ids * CAP + slot_rank, in_flight * CAP).astype(jnp.int32)


def group_sum(left_rows, right_rows):
    left_groups = left_rows.reshape(GROUPS, -1, left_rows.shape[1]).astype(jnp.float32)
    right_groups = right_rows.reshape(GROUPS, -1, right_rows.shape[1]).astype(jnp.float32)
    partial_sums = jnp.einsum("gri,grf->gif", left_groups, right_groups)
    rounded = lax.optimization_barrier(partial_sums.astype(jnp.bfloat16))
    return jnp.sum(rounded.astype(jnp.float32), axis=0)


def reference(tokens, cotangent, expert_ids, drop_mask, gate_table, gate_weight, up_weight, down_weight):
    blocks = TOKENS // TOK_DEV
    per_block = FLIGHT * CAP
    buffer_rows = blocks * per_block
    part_width = FF // SPLIT
    local = slot_table(expert_ids, drop_mask, TOK_DEV, FLIGHT)
    block_of = (jnp.arange(TOKENS, dtype=jnp.int32) // TOK_DEV)[:, None]
    token_of = jnp.broadcast_to(jnp.arange(TOKENS, dtype=jnp.int32)[:, None], (TOKENS, TOP))
    global_slot = jnp.where(local < per_block, block_of * per_block + local, buffer_rows).astype(jnp.int32).reshape(-1)
    slot_token = jnp.zeros((buffer_rows,), jnp.int32).at[global_slot].set(token_of.reshape(-1), mode="drop")
    slot_gate = jnp.zeros((buffer_rows,), jnp.float32).at[global_slot].set(gate_table.reshape(-1).astype(jnp.float32), mode="drop")
    filled = jnp.zeros((buffer_rows,), jnp.float32).at[global_slot].set(1.0, mode="drop")
    expert_in = jnp.where(filled[:, None] > 0, tokens[slot_token], jnp.zeros((), tokens.dtype))
    expert_grad = (slot_gate[:, None] * cotangent[slot_token].astype(jnp.float32)).astype(jnp.bfloat16)
    expert_in = expert_in.reshape(blocks, FLIGHT, CAP, D)
    expert_grad = expert_grad.reshape(blocks, FLIGHT, CAP, D)
    slot_grads = []
    gate_grads = []
    up_grads = []
    down_grads = []
    for expert in range(FLIGHT):
        rows_in = expert_in[:, expert].reshape(-1, D)
        rows_grad = expert_grad[:, expert].reshape(-1, D)
        gate_cols = gate_weight[:, expert * FF:(expert + 1) * FF]
        up_cols = up_weight[:, expert * FF:(expert + 1) * FF]
        down_rows = down_weight[expert * FF:(expert + 1) * FF, :]
        pre_gate = jnp.dot(rows_in, gate_cols, preferred_element_type=jnp.float32)
        pre_up = jnp.dot(rows_in, up_cols, preferred_element_type=jnp.float32)
        silu_value, silu_slope = silu_parts(pre_gate)
        activated = (silu_value * pre_up).astype(jnp.bfloat16)
        grad_act = jnp.dot(rows_grad, down_rows.T, preferred_element_type=jnp.float32)
        grad_gate_pre = (grad_act * pre_up * silu_slope).astype(jnp.bfloat16)
        grad_up_pre = (grad_act * silu_value).astype(jnp.bfloat16)
        slot_grad = jnp.zeros((rows_in.shape[0], D), jnp.float32)
        for part in range(SPLIT):
            low = part * part_width
            high = low + part_width
            slot_part = jnp.dot(grad_gate_pre[:, low:high], gate_cols[:, low:high].T, preferred_element_type=jnp.float32) + jnp.dot(grad_up_pre[:, low:high], up_cols[:, low:high].T, preferred_element_type=jnp.float32)
            slot_grad = slot_grad + slot_part.astype(jnp.bfloat16).astype(jnp.float32)
        slot_grads.append(slot_grad.reshape(blocks, CAP, D))
        gate_grads.append(group_sum(rows_in, grad_gate_pre))
        up_grads.append(group_sum(rows_in, grad_up_pre))
        down_grads.append(group_sum(activated, rows_grad))
    all_slots = jnp.stack(slot_grads, axis=1).reshape(buffer_rows, D)
    grad_tokens = jnp.zeros((TOKENS, D), jnp.float32).at[slot_token].add(all_slots * filled[:, None])
    return (grad_tokens.astype(jnp.bfloat16), jnp.concatenate(gate_grads, axis=1), jnp.concatenate(up_grads, axis=1), jnp.concatenate(down_grads, axis=0))
```

```python
import functools

import jax
import jax.numpy as jnp
from jax import lax
from jax.experimental import pallas as pl
from jax.experimental.pallas import tpu as pltpu
from jax.sharding import PartitionSpec as P

SPLIT = 4
CAP = 16
VMEM_LIMIT = 48 * 1024 * 1024

CONTRACT_LAST = (((1,), (1,)), ((), ()))
CONTRACT_FIRST = (((0,), (0,)), ((), ()))
PLAIN = (((1,), (0,)), ((), ()))


def dot(left, right, dims):
    return lax.dot_general(left, right, dims, preferred_element_type=jnp.float32)


def call(kernel, out_shape, args, after=(), flops=0):
    def run(*refs):
        kernel(*refs[: len(args)], *refs[len(args) + len(after) :])

    return pl.pallas_call(
        run,
        out_shape=out_shape,
        in_specs=[pl.BlockSpec(memory_space=pltpu.VMEM)] * len(args)
        + [pl.BlockSpec(memory_space=pl.ANY)] * len(after),
        out_specs=jax.tree.map(lambda _: pl.BlockSpec(memory_space=pltpu.VMEM), out_shape),
        compiler_params=pltpu.CompilerParams(vmem_limit_bytes=VMEM_LIMIT),
        cost_estimate=pl.CostEstimate(flops=flops, bytes_accessed=0, transcendentals=0),
    )(*args, *after)


def swap(values, axis, shift):
    size = lax.axis_size(axis)
    return lax.ppermute(values, axis, [(i, i ^ shift) for i in range(size)])


def begin_kernel(
    ids_hbm, mask_hbm, gate_hbm, tok_hbm, cot_hbm, gate_w_hbm, up_w_hbm, down_w_hbm,
    rows_ref, hot_ref, stack_ref,
    ids_ref, mask_ref, gate_ref, tok_ref, cot_ref, sems,
):
    flight, _, blocks, cap, width = rows_ref.shape
    hidden = gate_w_hbm.shape[0]
    pairs = [
        (ids_hbm, ids_ref),
        (mask_hbm, mask_ref),
        (gate_hbm, gate_ref),
        (tok_hbm, tok_ref),
        (cot_hbm, cot_ref),
        (gate_w_hbm, stack_ref.at[pl.ds(0, hidden)]),
        (up_w_hbm, stack_ref.at[pl.ds(hidden, hidden)]),
        (down_w_hbm, stack_ref.at[pl.ds(2 * hidden, hidden)]),
    ]
    copies = [
        pltpu.make_async_copy(source, target, sems.at[i])
        for i, (source, target) in enumerate(pairs)
    ]
    for copy in copies:
        copy.start()
    count = ids_ref.shape[1]
    earlier = (
        lax.broadcasted_iota(jnp.int32, (count, count), 0)
        < lax.broadcasted_iota(jnp.int32, (count, count), 1)
    ).astype(jnp.bfloat16)
    slot = lax.broadcasted_iota(jnp.int32, (cap, count), 0).astype(jnp.float32)
    for copy in copies[:5]:
        copy.wait()
    live = mask_ref[...] == 1
    for j in range(flight):
        hit = jnp.where((ids_ref[...] == j) & live, 1.0, 0.0)
        held = jnp.sum(hit, axis=0, keepdims=True)
        rank = jnp.sum(dot(hit.astype(jnp.bfloat16), earlier, PLAIN), axis=0, keepdims=True)
        gate = jnp.sum(hit * gate_ref[...], axis=0, keepdims=True)
        hot = jnp.where((slot == rank) & (held > 0.0), 1.0, 0.0)
        slot_gate = jnp.sum(hot * gate, axis=1, keepdims=True)
        hot = hot.astype(jnp.bfloat16)
        hot_ref[j] = hot
        picked = dot(hot, tok_ref[...], PLAIN).astype(jnp.bfloat16)
        graded = (slot_gate * dot(hot, cot_ref[...], PLAIN)).astype(jnp.bfloat16)
        for b in range(blocks):
            rows_ref[j, 0, b] = picked[:, b * width : (b + 1) * width]
            rows_ref[j, 1, b] = graded[:, b * width : (b + 1) * width]
    for copy in copies[5:]:
        copy.wait()


def join_kernel(*refs):
    for i, ref in enumerate(refs[:-1]):
        refs[-1][i] = ref[...]


def rows_of(row_refs, kind, block):
    return jnp.concatenate([r[kind, block] for r in row_refs], axis=0)


def repack_kernel(chunks, *refs):
    me = lax.axis_index("dp")
    for i, out_ref in enumerate(refs[chunks:]):
        first = ((me ^ (2 * i)) // 2) * 2
        for kind in range(2):
            for k in range(2):
                out_ref[kind, k] = rows_of(refs[:chunks], kind, first + k)


def expert_kernel(chunks, *refs):
    row_refs, (half_ref, other_ref, grads_ref) = refs[:chunks], refs[chunks : chunks + 3]
    part_refs = refs[chunks + 3 :]
    me = lax.axis_index("dp")
    blocks = 2 * half_ref.shape[0]
    weight_refs = [(half_ref, other_ref)[s % 2].at[s // 2] for s in range(blocks)]
    hidden = weight_refs[0].shape[0] // 3
    pre_gate, pre_up, grad_act = 0.0, 0.0, 0.0
    for s, weight_ref in enumerate(weight_refs):
        rows_in = rows_of(row_refs, 0, me ^ s)
        pre_gate += dot(rows_in, weight_ref[:hidden], CONTRACT_LAST)
        pre_up += dot(rows_in, weight_ref[hidden : 2 * hidden], CONTRACT_LAST)
        rows_grad = rows_of(row_refs, 1, me ^ s)
        grad_act += dot(rows_grad, weight_ref[2 * hidden :], CONTRACT_LAST)
    sigmoid_value = lax.logistic(pre_gate)
    silu_value = pre_gate * sigmoid_value
    slope = sigmoid_value * (1.0 + pre_gate * (1.0 - sigmoid_value))
    grad_gate_pre = (grad_act * pre_up * slope).astype(jnp.bfloat16)
    grad_up_pre = (grad_act * silu_value).astype(jnp.bfloat16)
    activated = (silu_value * pre_up).astype(jnp.bfloat16)
    grads_ref[...] = jnp.concatenate([grad_gate_pre, grad_up_pre, activated], axis=1)
    for s, weight_ref in enumerate(weight_refs):
        part = dot(grad_gate_pre, weight_ref[:hidden], PLAIN)
        part += dot(grad_up_pre, weight_ref[hidden : 2 * hidden], PLAIN)
        part = part.astype(jnp.bfloat16)
        for c, part_ref in enumerate(part_refs):
            part_ref[me ^ s] = part[c * CAP : (c + 1) * CAP]


def weight_grad_kernel(chips, *refs):
    row_refs, grad_refs = refs[:chips], refs[chips : 2 * chips]
    own_ref, other_ref = refs[-2:]
    hidden = own_ref.shape[0] // 3
    core = lax.rem(lax.axis_index("dp"), 2)
    grads = jnp.concatenate([g[...] for g in grad_refs], axis=0)
    for out_ref, block in ((other_ref, 1 - core), (own_ref, core)):
        rows_in = jnp.concatenate([r[0, block] for r in row_refs], axis=0)
        rows_grad = jnp.concatenate([r[1, block] for r in row_refs], axis=0)
        pair = dot(grads[:, : 2 * hidden], rows_in, CONTRACT_FIRST)
        down = dot(grads[:, 2 * hidden :], rows_grad, CONTRACT_FIRST)
        out_ref[: 2 * hidden] = pair.astype(out_ref.dtype)
        out_ref[2 * hidden :] = down.astype(out_ref.dtype)


def finish_kernel(own_ref, other_ref, gate_ref, up_ref, down_ref):
    hidden = gate_ref.shape[0]
    for i, out_ref in enumerate((gate_ref, up_ref, down_ref)):
        part = slice(i * hidden, (i + 1) * hidden)
        out_ref[...] = own_ref[part] + other_ref[part].astype(jnp.float32)


def place_kernel(chunks, hot_ref, *refs):
    part_refs, out_ref = refs[:chunks], refs[chunks]
    flight = hot_ref.shape[0]
    blocks, _, width = part_refs[0].shape
    home = lax.axis_index("expert") // SPLIT
    for b in range(blocks):
        total = 0.0
        for j in range(flight):
            summed = 0.0
            for c in range(j * SPLIT, (j + 1) * SPLIT):
                summed += part_refs[c][b].astype(jnp.float32)
            high = summed.astype(jnp.bfloat16)
            hot = hot_ref[home ^ j]
            total += dot(hot, high, CONTRACT_FIRST)
            if flight > 1:
                low = (summed - high.astype(jnp.float32)).astype(jnp.bfloat16)
                total += dot(hot, low, CONTRACT_FIRST)
        out_ref[:, b * width : (b + 1) * width] = total.astype(out_ref.dtype)


def body(tokens, cotangent, expert_ids, drop_mask, gate_table, gate_weight, up_weight, down_weight):
    chunks = lax.axis_size("expert")
    blocks = lax.axis_size("dp")
    flight = chunks // SPLIT
    count, model_width = tokens.shape
    width = model_width // blocks
    hidden = gate_weight.shape[1]
    rows = chunks * CAP
    struct = jax.ShapeDtypeStruct

    chips = blocks // 2
    dma = pltpu.SemaphoreType.DMA
    operands = (
        expert_ids.T, drop_mask.T, gate_table.T, tokens, cotangent,
        gate_weight.T, up_weight.T, down_weight,
    )
    own_rows, hot, own_weights = pl.pallas_call(
        begin_kernel,
        out_shape=(
            struct((flight, 2, blocks, CAP, width), jnp.bfloat16),
            struct((flight, CAP, count), jnp.bfloat16),
            struct((3 * hidden, width), jnp.bfloat16),
        ),
        in_specs=[pl.BlockSpec(memory_space=pltpu.HBM)] * 8,
        out_specs=(pl.BlockSpec(memory_space=pltpu.VMEM),) * 3,
        scratch_shapes=[pltpu.VMEM(v.shape, v.dtype) for v in operands[:5]] + [dma((8,))],
        compiler_params=pltpu.CompilerParams(vmem_limit_bytes=VMEM_LIMIT),
    )(*[pltpu.with_memory_space_constraint(v, pltpu.HBM) for v in operands])
    me = lax.axis_index("expert")

    def rows_for(c):
        if flight == 1:
            return own_rows[0]
        return lax.dynamic_index_in_dim(own_rows, (me ^ c) // SPLIT, 0, keepdims=False)

    arrived = [rows_for(0)]
    for c in range(1, chunks):
        if c % SPLIT == 3:
            arrived.append(swap(arrived[c - 1], "expert", 1))
        else:
            arrived.append(swap(rows_for(c), "expert", c))
    shards = [swap(own_weights, "dp", 2 * i) for i in reversed(range(1, chips))]
    shards = [own_weights] + shards[::-1]
    half = call(
        join_kernel,
        struct((chips, 3 * hidden, width), jnp.bfloat16),
        shards,
        after=arrived[1:],
    )
    other_half = swap(half, "dp", 1)
    packed = call(
        functools.partial(repack_kernel, chunks),
        [struct((2, 2, rows, width), jnp.bfloat16)] * chips,
        arrived,
    )
    block_rows = [packed[0]] + [swap(packed[i], "dp", 2 * i) for i in range(1, chips)]

    grads, *parts = call(
        functools.partial(expert_kernel, chunks),
        [struct((rows, 3 * hidden), jnp.bfloat16)]
        + [struct((blocks, CAP, width), jnp.bfloat16)] * chunks,
        (*arrived, half, other_half),
        flops=5 * 10**9,
    )
    all_grads = [grads] + [swap(grads, "dp", 2 * i) for i in range(1, chips)]
    returned = [parts[0]] + [swap(parts[c], "expert", c) for c in range(1, chunks)]

    own_sum, other_sum = call(
        functools.partial(weight_grad_kernel, chips),
        [
            struct((3 * hidden, width), jnp.float32),
            struct((3 * hidden, width), jnp.bfloat16),
        ],
        (*block_rows, *all_grads),
        after=returned[1:],
    )
    other_sum = swap(other_sum, "dp", 1)
    grad_tokens = call(
        functools.partial(place_kernel, chunks),
        struct((count, model_width), jnp.bfloat16),
        (hot, *returned),
    )
    grad_gate, grad_up, grad_down = call(
        finish_kernel,
        [struct((hidden, width), jnp.float32)] * 3,
        (own_sum, other_sum),
    )
    return grad_tokens, grad_gate.T, grad_up.T, grad_down


def solution(mesh):
    split_rows = P(("dp", "expert"), None)
    return jax.shard_map(
        body,
        mesh=mesh,
        in_specs=(split_rows,) * 5 + (P("dp", "expert"), P("dp", "expert"), P("expert", "dp")),
        out_specs=(split_rows, P("dp", "expert"), P("dp", "expert"), P("expert", "dp")),
        check_vma=False,
    )
```

```python
import functools

import jax
import jax.numpy as jnp
from jax import lax
from jax.experimental import pallas as pl
from jax.experimental.pallas import tpu as pltpu
from jax.sharding import PartitionSpec as P

SPLIT = 4
CAP = 16
SINGLE = 3
VMEM_LIMIT = 48 * 1024 * 1024

CONTRACT_LAST = (((1,), (1,)), ((), ()))
CONTRACT_FIRST = (((0,), (0,)), ((), ()))
PLAIN = (((1,), (0,)), ((), ()))


def dot(left, right, dims):
    return lax.dot_general(left, right, dims, preferred_element_type=jnp.float32)


def call(kernel, out_shape, args, after=(), flops=0):
    def run(*refs):
        kernel(*refs[: len(args)], *refs[len(args) + len(after) :])

    return pl.pallas_call(
        run,
        out_shape=out_shape,
        in_specs=[pl.BlockSpec(memory_space=pltpu.VMEM)] * len(args)
        + [pl.BlockSpec(memory_space=pl.ANY)] * len(after),
        out_specs=jax.tree.map(lambda _: pl.BlockSpec(memory_space=pltpu.VMEM), out_shape),
        compiler_params=pltpu.CompilerParams(vmem_limit_bytes=VMEM_LIMIT),
        cost_estimate=pl.CostEstimate(flops=flops, bytes_accessed=0, transcendentals=0),
    )(*args, *after)


def swap(values, axis, shift):
    size = lax.axis_size(axis)
    return lax.ppermute(values, axis, [(i, i ^ shift) for i in range(size)])


def cross(values, pair):
    size = lax.axis_size("dp")
    return lax.ppermute(values, "dp", [(i, i ^ (2 * pair[i % 2])) for i in range(size)])


def begin_kernel(
    ids_hbm, mask_hbm, gate_hbm, tok_hbm, cot_hbm, gate_w_hbm, up_w_hbm, down_w_hbm,
    rows_ref, hot_ref, stack_ref,
    ids_ref, mask_ref, gate_ref, tok_ref, cot_ref, sems,
):
    flight, _, blocks, cap, width = rows_ref.shape
    hidden = gate_w_hbm.shape[0]
    pairs = [
        (ids_hbm, ids_ref),
        (mask_hbm, mask_ref),
        (gate_hbm, gate_ref),
        (tok_hbm, tok_ref),
        (cot_hbm, cot_ref),
        (gate_w_hbm, stack_ref.at[pl.ds(0, hidden)]),
        (up_w_hbm, stack_ref.at[pl.ds(hidden, hidden)]),
        (down_w_hbm, stack_ref.at[pl.ds(2 * hidden, hidden)]),
    ]
    copies = [
        pltpu.make_async_copy(source, target, sems.at[i])
        for i, (source, target) in enumerate(pairs)
    ]
    for copy in copies:
        copy.start()
    count = ids_ref.shape[1]
    earlier = (
        lax.broadcasted_iota(jnp.int32, (count, count), 0)
        < lax.broadcasted_iota(jnp.int32, (count, count), 1)
    ).astype(jnp.bfloat16)
    slot = lax.broadcasted_iota(jnp.int32, (cap, count), 0).astype(jnp.float32)
    for copy in copies[:3]:
        copy.wait()
    live = mask_ref[...] == 1
    gates = []
    for j in range(flight):
        hit = jnp.where((ids_ref[...] == j) & live, 1.0, 0.0)
        held = jnp.sum(hit, axis=0, keepdims=True)
        rank = jnp.sum(dot(hit.astype(jnp.bfloat16), earlier, PLAIN), axis=0, keepdims=True)
        gate = jnp.sum(hit * gate_ref[...], axis=0, keepdims=True)
        hot = jnp.where((slot == rank) & (held > 0.0), 1.0, 0.0)
        gates.append(jnp.sum(hot * gate, axis=1, keepdims=True))
        hot_ref[j] = hot.astype(jnp.bfloat16)
    for copy in copies[3:5]:
        copy.wait()
    for j in range(flight):
        picked = dot(hot_ref[j], tok_ref[...], PLAIN).astype(jnp.bfloat16)
        graded = (gates[j] * dot(hot_ref[j], cot_ref[...], PLAIN)).astype(jnp.bfloat16)
        for b in range(blocks):
            rows_ref[j, 0, b] = picked[:, b * width : (b + 1) * width]
            rows_ref[j, 1, b] = graded[:, b * width : (b + 1) * width]
    for copy in copies[5:]:
        copy.wait()


def join_kernel(*refs):
    out_ref, low = refs[-1], 0
    for ref in refs[:-1]:
        out_ref[low : low + ref.shape[0]] = ref[...]
        low += ref.shape[0]


def join_rows_kernel(first_ref, second_ref, out_ref):
    size = first_ref.shape[2]
    out_ref[:, :, :size] = first_ref[...]
    out_ref[:, :, size:] = second_ref[...]


def rows_of(row_refs, kind, block):
    return jnp.concatenate([r[kind, block] for r in row_refs], axis=0)


def own_shift(me, pair):
    first = lax.rem(me, 2) == 0
    return [2 * jnp.where(first, pair[i], pair[1 - i]) for i in range(2)]


def repack_kernel(chunks, pairs, *refs):
    me = lax.axis_index("dp")
    shifts = [0, 2 * SINGLE]
    for pair in pairs:
        mine, other = own_shift(me, pair)
        shifts += [mine, other ^ 1]
    for shift, out_ref in zip(shifts, refs[chunks:]):
        for kind in range(2):
            for k in range(2):
                out_ref[kind, k] = rows_of(refs[:chunks], kind, me ^ shift ^ k)


def expert_kernel(chunks, *refs):
    row_refs, (half_ref, other_ref, grads_ref) = refs[:chunks], refs[chunks : chunks + 3]
    near_part_ref, far_part_ref = refs[chunks + 3 :]
    flight = chunks // SPLIT
    me = lax.axis_index("dp")
    weights = []
    for i in range(half_ref.shape[0]):
        weights += [(half_ref.at[i], me ^ (2 * i)), (other_ref.at[i], me ^ (2 * i + 1))]
    hidden = half_ref.shape[1] // 3
    pre_gate, pre_up, grad_act = 0.0, 0.0, 0.0
    for weight_ref, block in weights:
        rows_in = rows_of(row_refs, 0, block)
        pre_gate += dot(rows_in, weight_ref[:hidden], CONTRACT_LAST)
        pre_up += dot(rows_in, weight_ref[hidden : 2 * hidden], CONTRACT_LAST)
        grad_act += dot(rows_of(row_refs, 1, block), weight_ref[2 * hidden :], CONTRACT_LAST)
    sigmoid_value = lax.logistic(pre_gate)
    silu_value = pre_gate * sigmoid_value
    slope = sigmoid_value * (1.0 + pre_gate * (1.0 - sigmoid_value))
    grad_gate_pre = (grad_act * pre_up * slope).astype(jnp.bfloat16)
    grad_up_pre = (grad_act * silu_value).astype(jnp.bfloat16)
    activated = (silu_value * pre_up).astype(jnp.bfloat16)
    grads_ref[...] = jnp.concatenate([grad_gate_pre, grad_up_pre, activated], axis=1)
    for weight_ref, block in weights:
        part = dot(grad_gate_pre, weight_ref[:hidden], PLAIN)
        part += dot(grad_up_pre, weight_ref[hidden : 2 * hidden], PLAIN)
        part = part.astype(jnp.bfloat16)
        for j in range(flight):
            for half, first in ((0, 0), (flight, 2)):
                low = (SPLIT * j + first) * CAP
                near_part_ref[half + j, block] = part[low : low + CAP]
                far_part_ref[half + j, block] = part[low + CAP : low + 2 * CAP]


def weight_grad_kernel(sibling, *refs):
    out_ref, half = refs[-1], (len(refs) - 1) // 2
    row_refs, grad_refs = refs[:half], refs[half:-1]
    hidden = out_ref.shape[0] // 3
    grads = jnp.concatenate([g[...] for g in grad_refs], axis=0)
    rows_in = jnp.concatenate([r[0, sibling] for r in row_refs], axis=0)
    rows_grad = jnp.concatenate([r[1, sibling] for r in row_refs], axis=0)
    pair = dot(grads[:, : 2 * hidden], rows_in, CONTRACT_FIRST)
    down = dot(grads[:, 2 * hidden :], rows_grad, CONTRACT_FIRST)
    out_ref[: 2 * hidden] = pair.astype(out_ref.dtype)
    out_ref[2 * hidden :] = down.astype(out_ref.dtype)


def add_kernel(near_ref, far_ref, out_ref):
    half = out_ref.shape[0]
    total = near_ref[half:].astype(jnp.float32) + far_ref[half:].astype(jnp.float32)
    out_ref[...] = total.astype(out_ref.dtype)


def sum_kernel(near_ref, far_ref, pair_ref, out_ref):
    half = out_ref.shape[0]
    total = near_ref[:half].astype(jnp.float32) + far_ref[:half].astype(jnp.float32)
    out_ref[...] = (total + pair_ref[...].astype(jnp.float32)).astype(out_ref.dtype)


def finish_kernel(chunks, own_ref, other_ref, hot_ref, *refs):
    part_refs, refs = refs[:chunks], refs[chunks:]
    out_hbm, *grad_hbm = refs[:4]
    out_ref, grad_ref, sems = refs[4:]
    hidden = grad_hbm[0].shape[0]
    copies = []

    def send(source, target):
        copies.append(pltpu.make_async_copy(source, target, sems.at[len(copies)]))
        copies[-1].start()

    for i, hbm in enumerate(grad_hbm):
        part = pl.ds(i * hidden, hidden)
        grad_ref[part] = own_ref[part] + other_ref[part].astype(jnp.float32)
        send(grad_ref.at[part], hbm)
    flight = hot_ref.shape[0]
    blocks, _, width = part_refs[0].shape[-3:]
    step = blocks * width // 4
    home = lax.axis_index("expert") // SPLIT
    for b in range(blocks):
        total = 0.0
        for j in range(flight):
            if flight == 1:
                near_ref, far_ref, pair_ref = part_refs
                summed = near_ref[0, b].astype(jnp.float32) + far_ref[0, b].astype(jnp.float32)
                summed = (summed + pair_ref[0, b].astype(jnp.float32)).astype(jnp.bfloat16)
            else:
                summed = part_refs[j][b]
            total += dot(hot_ref[home ^ j], summed, CONTRACT_FIRST)
        out_ref[:, b * width : (b + 1) * width] = total.astype(out_ref.dtype)
        if (b + 1) * width % step == 0:
            columns = pl.ds((b + 1) * width - step, step)
            send(out_ref.at[:, columns], out_hbm.at[:, columns])
    for copy in copies:
        copy.wait()


def body(tokens, cotangent, expert_ids, drop_mask, gate_table, gate_weight, up_weight, down_weight):
    chunks = lax.axis_size("expert")
    blocks = lax.axis_size("dp")
    flight = chunks // SPLIT
    count, model_width = tokens.shape
    width = model_width // blocks
    hidden = gate_weight.shape[1]
    rows = chunks * CAP
    struct = jax.ShapeDtypeStruct

    chips = blocks // 2
    dma = pltpu.SemaphoreType.DMA
    operands = (
        expert_ids.T, drop_mask.T, gate_table.T, tokens, cotangent,
        gate_weight.T, up_weight.T, down_weight,
    )
    own_rows, hot, own_weights = pl.pallas_call(
        begin_kernel,
        out_shape=(
            struct((flight, 2, blocks, CAP, width), jnp.bfloat16),
            struct((flight, CAP, count), jnp.bfloat16),
            struct((3 * hidden, width), jnp.bfloat16),
        ),
        in_specs=[pl.BlockSpec(memory_space=pltpu.HBM)] * 8,
        out_specs=(pl.BlockSpec(memory_space=pltpu.VMEM),) * 3,
        scratch_shapes=[pltpu.VMEM(v.shape, v.dtype) for v in operands[:5]] + [dma((8,))],
        compiler_params=pltpu.CompilerParams(vmem_limit_bytes=VMEM_LIMIT),
    )(*[pltpu.with_memory_space_constraint(v, pltpu.HBM) for v in operands])
    me = lax.axis_index("expert")

    def rows_for(c):
        if flight == 1:
            return own_rows[0]
        return lax.dynamic_index_in_dim(own_rows, (me ^ c) // SPLIT, 0, keepdims=False)

    arrived = [rows_for(0)]
    for c in range(1, chunks):
        if c % SPLIT == 3:
            arrived.append(swap(arrived[c - 1], "expert", 1))
        else:
            arrived.append(swap(rows_for(c), "expert", c))
    pairs = [(1, 2)] + [(i, i + 1) for i in range(4, chips, 2)]
    shards = [swap(own_weights, "dp", 2 * i) for i in reversed(range(1, chips))]
    half = call(
        join_kernel,
        struct((chips, 3 * hidden, width), jnp.bfloat16),
        [v[None] for v in (own_weights, *shards[::-1])],
        after=arrived[1:],
    )
    other_half = swap(half, "dp", 1)
    rows_shape = (2, 2, rows, width)
    own_block, single_block, *packed = call(
        functools.partial(repack_kernel, chunks, pairs),
        [struct(rows_shape, jnp.bfloat16)] * (2 + 2 * len(pairs)),
        arrived,
    )
    block_rows = [own_block, swap(single_block, "dp", 2 * SINGLE)]
    for n, pair in enumerate(pairs):
        mine, other = packed[2 * n : 2 * n + 2]
        both = call(
            join_rows_kernel,
            struct((2, 2, 2 * rows, width), jnp.bfloat16),
            (mine, swap(other, "dp", 1)),
        )
        block_rows.append(cross(both, pair))

    grads, near_parts, far_parts = call(
        functools.partial(expert_kernel, chunks),
        [struct((rows, 3 * hidden), jnp.bfloat16)]
        + [struct((2 * flight, blocks, CAP, width), jnp.bfloat16)] * 2,
        (*arrived, half, other_half),
        flops=5 * 10**9,
    )
    chip_grads = call(
        join_kernel,
        struct((2 * rows, 3 * hidden), jnp.bfloat16),
        (grads, swap(grads, "dp", 1)),
    )
    all_grads = [grads, swap(grads, "dp", 2 * SINGLE)]
    all_grads += [cross(chip_grads, pair) for pair in pairs]
    far_parts = swap(far_parts, "expert", 1)
    pair = struct((flight, blocks, CAP, width), jnp.bfloat16)
    pair_sum = call(add_kernel, pair, (near_parts, far_parts), after=block_rows[1:], flops=3 * 10**9)
    half_sum, pair_sum = pair_sum, swap(pair_sum, "expert", 2)
    returned = (near_parts, far_parts, pair_sum)
    if flight > 1:
        slot_grad = call(sum_kernel, pair, returned)
        returned = [slot_grad[0]]
        returned += [swap(slot_grad[j], "expert", SPLIT * j) for j in range(1, flight)]

    terms = (*block_rows, *all_grads)
    other_sum = call(
        functools.partial(weight_grad_kernel, 1),
        struct((3 * hidden, width), jnp.bfloat16),
        terms,
        after=(half_sum,),
        flops=10**10,
    )
    own_sum = call(
        functools.partial(weight_grad_kernel, 0),
        struct((3 * hidden, width), jnp.float32),
        terms,
        after=(other_sum,),
        flops=10**10,
    )
    other_sum = swap(other_sum, "dp", 1)
    grad_tokens, grad_gate, grad_up, grad_down = pl.pallas_call(
        functools.partial(finish_kernel, len(returned)),
        out_shape=[struct((count, model_width), jnp.bfloat16)]
        + [struct((hidden, width), jnp.float32)] * 3,
        in_specs=[pl.BlockSpec(memory_space=pltpu.VMEM)] * (3 + len(returned)),
        out_specs=[pl.BlockSpec(memory_space=pltpu.HBM)] * 4,
        scratch_shapes=[
            pltpu.VMEM((count, model_width), jnp.bfloat16),
            pltpu.VMEM((3 * hidden, width), jnp.float32),
            dma((7,)),
        ],
        compiler_params=pltpu.CompilerParams(vmem_limit_bytes=VMEM_LIMIT),
    )(own_sum, other_sum, hot, *returned)
    return grad_tokens, grad_gate.T, grad_up.T, grad_down


def solution(mesh):
    split_rows = P(("dp", "expert"), None)
    return jax.shard_map(
        body,
        mesh=mesh,
        in_specs=(split_rows,) * 5 + (P("dp", "expert"), P("dp", "expert"), P("expert", "dp")),
        out_specs=(split_rows, P("dp", "expert"), P("dp", "expert"), P("expert", "dp")),
        check_vma=False,
    )
```

```python
import functools

import jax
import jax.numpy as jnp
from jax import lax
from jax.experimental import pallas as pl
from jax.experimental.pallas import tpu as pltpu
from jax.sharding import PartitionSpec as P

SPLIT = 4
CAP = 16
SINGLE = 3
VMEM_LIMIT = 48 * 1024 * 1024

CONTRACT_LAST = (((1,), (1,)), ((), ()))
CONTRACT_FIRST = (((0,), (0,)), ((), ()))
PLAIN = (((1,), (0,)), ((), ()))


def dot(left, right, dims):
    return lax.dot_general(left, right, dims, preferred_element_type=jnp.float32)


def call(kernel, out_shape, args, after=(), flops=0):
    def run(*refs):
        kernel(*refs[: len(args)], *refs[len(args) + len(after) :])

    return pl.pallas_call(
        run,
        out_shape=out_shape,
        in_specs=[pl.BlockSpec(memory_space=pltpu.VMEM)] * len(args)
        + [pl.BlockSpec(memory_space=pl.ANY)] * len(after),
        out_specs=jax.tree.map(lambda _: pl.BlockSpec(memory_space=pltpu.VMEM), out_shape),
        compiler_params=pltpu.CompilerParams(vmem_limit_bytes=VMEM_LIMIT),
        cost_estimate=pl.CostEstimate(flops=flops, bytes_accessed=0, transcendentals=0),
    )(*args, *after)


def swap(values, axis, shift):
    size = lax.axis_size(axis)
    return lax.ppermute(values, axis, [(i, i ^ shift) for i in range(size)])


def cross(values, pair):
    size = lax.axis_size("dp")
    return lax.ppermute(values, "dp", [(i, i ^ (2 * pair[i % 2])) for i in range(size)])


def begin_kernel(
    ids_hbm, mask_hbm, gate_hbm, tok_hbm, cot_hbm, gate_w_hbm, up_w_hbm, down_w_hbm,
    rows_ref, hot_ref, stack_ref,
    ids_ref, mask_ref, gate_ref, tok_ref, cot_ref, sems,
):
    flight, _, blocks, cap, width = rows_ref.shape
    hidden = gate_w_hbm.shape[0]
    pairs = [
        (ids_hbm, ids_ref),
        (mask_hbm, mask_ref),
        (gate_hbm, gate_ref),
        (tok_hbm, tok_ref),
        (cot_hbm, cot_ref),
        (gate_w_hbm, stack_ref.at[pl.ds(0, hidden)]),
        (up_w_hbm, stack_ref.at[pl.ds(hidden, hidden)]),
        (down_w_hbm, stack_ref.at[pl.ds(2 * hidden, hidden)]),
    ]
    copies = [
        pltpu.make_async_copy(source, target, sems.at[i])
        for i, (source, target) in enumerate(pairs)
    ]
    for copy in copies:
        copy.start()
    count = ids_ref.shape[1]
    earlier = (
        lax.broadcasted_iota(jnp.int32, (count, count), 0)
        < lax.broadcasted_iota(jnp.int32, (count, count), 1)
    ).astype(jnp.bfloat16)
    slot = lax.broadcasted_iota(jnp.int32, (cap, count), 0).astype(jnp.float32)
    for copy in copies[:3]:
        copy.wait()
    live = mask_ref[...] == 1
    gates = []
    for j in range(flight):
        hit = jnp.where((ids_ref[...] == j) & live, 1.0, 0.0)
        held = jnp.sum(hit, axis=0, keepdims=True)
        rank = jnp.sum(dot(hit.astype(jnp.bfloat16), earlier, PLAIN), axis=0, keepdims=True)
        gate = jnp.sum(hit * gate_ref[...], axis=0, keepdims=True)
        hot = jnp.where((slot == rank) & (held > 0.0), 1.0, 0.0)
        gates.append(jnp.sum(hot * gate, axis=1, keepdims=True))
        hot_ref[j] = hot.astype(jnp.bfloat16)
    for copy in copies[3:5]:
        copy.wait()
    for j in range(flight):
        picked = dot(hot_ref[j], tok_ref[...], PLAIN).astype(jnp.bfloat16)
        graded = (gates[j] * dot(hot_ref[j], cot_ref[...], PLAIN)).astype(jnp.bfloat16)
        for b in range(blocks):
            rows_ref[j, 0, b] = picked[:, b * width : (b + 1) * width]
            rows_ref[j, 1, b] = graded[:, b * width : (b + 1) * width]
    for copy in copies[5:]:
        copy.wait()


def join_kernel(*refs):
    out_ref, low = refs[-1], 0
    for ref in refs[:-1]:
        out_ref[low : low + ref.shape[0]] = ref[...]
        low += ref.shape[0]


def join_rows_kernel(first_ref, second_ref, out_ref):
    size = first_ref.shape[2]
    out_ref[:, :, :size] = first_ref[...]
    out_ref[:, :, size:] = second_ref[...]


def rows_of(row_refs, kind, block):
    return jnp.concatenate([r[kind, block] for r in row_refs], axis=0)


def own_shift(me, pair):
    first = lax.rem(me, 2) == 0
    return [2 * jnp.where(first, pair[i], pair[1 - i]) for i in range(2)]


def repack_kernel(chunks, pairs, *refs):
    me = lax.axis_index("dp")
    shifts = [0, 2 * SINGLE]
    for pair in pairs:
        mine, other = own_shift(me, pair)
        shifts += [mine, other ^ 1]
    for shift, out_ref in zip(shifts, refs[chunks:]):
        for kind in range(2):
            for k in range(2):
                out_ref[kind, k] = rows_of(refs[:chunks], kind, me ^ shift ^ k)


def expert_kernel(chunks, *refs):
    row_refs, (half_ref, other_ref, grads_ref) = refs[:chunks], refs[chunks : chunks + 3]
    near_ref, direct_ref, relay_ref = refs[chunks + 3 :]
    flight = chunks // SPLIT
    me = lax.axis_index("dp")
    weights = []
    for i in range(half_ref.shape[0]):
        weights += [(half_ref.at[i], me ^ (2 * i)), (other_ref.at[i], me ^ (2 * i + 1))]
    hidden = half_ref.shape[1] // 3
    pre_gate, pre_up, grad_act = 0.0, 0.0, 0.0
    for weight_ref, block in weights:
        rows_in = rows_of(row_refs, 0, block)
        pre_gate += dot(rows_in, weight_ref[:hidden], CONTRACT_LAST)
        pre_up += dot(rows_in, weight_ref[hidden : 2 * hidden], CONTRACT_LAST)
        grad_act += dot(rows_of(row_refs, 1, block), weight_ref[2 * hidden :], CONTRACT_LAST)
    sigmoid_value = lax.logistic(pre_gate)
    silu_value = pre_gate * sigmoid_value
    slope = sigmoid_value * (1.0 + pre_gate * (1.0 - sigmoid_value))
    grad_gate_pre = (grad_act * pre_up * slope).astype(jnp.bfloat16)
    grad_up_pre = (grad_act * silu_value).astype(jnp.bfloat16)
    activated = (silu_value * pre_up).astype(jnp.bfloat16)
    grads_ref[...] = jnp.concatenate([grad_gate_pre, grad_up_pre, activated], axis=1)
    for weight_ref, block in weights:
        part = dot(grad_gate_pre, weight_ref[:hidden], PLAIN)
        part += dot(grad_up_pre, weight_ref[hidden : 2 * hidden], PLAIN)
        part = part.astype(jnp.bfloat16)
        for j in range(flight):
            targets = ((near_ref, j), (direct_ref, j), (near_ref, flight + j), (relay_ref, j))
            for c, (part_ref, n) in enumerate(targets):
                low = (SPLIT * j + c) * CAP
                part_ref[n, block] = part[low : low + CAP]


def weight_grad_kernel(sibling, *refs):
    out_ref, half = refs[-1], (len(refs) - 1) // 2
    row_refs, grad_refs = refs[:half], refs[half:-1]
    hidden = out_ref.shape[0] // 3
    grads = jnp.concatenate([g[...] for g in grad_refs], axis=0)
    rows_in = jnp.concatenate([r[0, sibling] for r in row_refs], axis=0)
    rows_grad = jnp.concatenate([r[1, sibling] for r in row_refs], axis=0)
    pair = dot(grads[:, : 2 * hidden], rows_in, CONTRACT_FIRST)
    down = dot(grads[:, 2 * hidden :], rows_grad, CONTRACT_FIRST)
    out_ref[: 2 * hidden] = pair.astype(out_ref.dtype)
    out_ref[2 * hidden :] = down.astype(out_ref.dtype)


def add_kernel(near_ref, relay_ref, direct_ref, out_ref, direct_out_ref):
    direct_out_ref[...] = direct_ref[...]
    half = out_ref.shape[0]
    total = near_ref[half:].astype(jnp.float32) + relay_ref[...].astype(jnp.float32)
    out_ref[...] = total.astype(out_ref.dtype)


def sum_kernel(near_ref, pair_ref, direct_ref, out_ref):
    half = out_ref.shape[0]
    total = near_ref[:half].astype(jnp.float32) + direct_ref[...].astype(jnp.float32)
    out_ref[...] = (total + pair_ref[...].astype(jnp.float32)).astype(out_ref.dtype)


def finish_kernel(chunks, own_ref, other_ref, hot_ref, *refs):
    part_refs, refs = refs[:chunks], refs[chunks:]
    out_hbm, *grad_hbm = refs[:4]
    out_ref, grad_ref, sems = refs[4:]
    hidden = grad_hbm[0].shape[0]
    copies = []

    def send(source, target):
        copies.append(pltpu.make_async_copy(source, target, sems.at[len(copies)]))
        copies[-1].start()

    for i, hbm in enumerate(grad_hbm):
        part = pl.ds(i * hidden, hidden)
        grad_ref[part] = own_ref[part] + other_ref[part].astype(jnp.float32)
        send(grad_ref.at[part], hbm)
    flight = hot_ref.shape[0]
    blocks, _, width = part_refs[0].shape[-3:]
    home = lax.axis_index("expert") // SPLIT
    hots = [hot_ref[home ^ j].astype(jnp.float32).T.astype(jnp.bfloat16) for j in range(flight)]

    def slot_rows(j, b):
        if flight > 1:
            return part_refs[j][b]
        near_ref, pair_ref, direct_ref = part_refs
        total = near_ref[0, b].astype(jnp.float32) + direct_ref[0, b].astype(jnp.float32)
        return (total + pair_ref[0, b].astype(jnp.float32)).astype(jnp.bfloat16)

    step = blocks // 4
    for first in range(0, blocks, step):
        total = 0.0
        for j in range(flight):
            rows = [slot_rows(j, b) for b in range(first, first + step)]
            total += dot(hots[j], jnp.concatenate(rows, axis=1), PLAIN)
        columns = pl.ds(first * width, step * width)
        out_ref[:, columns] = total.astype(out_ref.dtype)
        send(out_ref.at[:, columns], out_hbm.at[:, columns])
    for copy in copies:
        copy.wait()


def body(tokens, cotangent, expert_ids, drop_mask, gate_table, gate_weight, up_weight, down_weight):
    chunks = lax.axis_size("expert")
    blocks = lax.axis_size("dp")
    flight = chunks // SPLIT
    count, model_width = tokens.shape
    width = model_width // blocks
    hidden = gate_weight.shape[1]
    rows = chunks * CAP
    struct = jax.ShapeDtypeStruct

    chips = blocks // 2
    dma = pltpu.SemaphoreType.DMA
    operands = (
        expert_ids.T, drop_mask.T, gate_table.T, tokens, cotangent,
        gate_weight.T, up_weight.T, down_weight,
    )
    own_rows, hot, own_weights = pl.pallas_call(
        begin_kernel,
        out_shape=(
            struct((flight, 2, blocks, CAP, width), jnp.bfloat16),
            struct((flight, CAP, count), jnp.bfloat16),
            struct((3 * hidden, width), jnp.bfloat16),
        ),
        in_specs=[pl.BlockSpec(memory_space=pltpu.HBM)] * 8,
        out_specs=(pl.BlockSpec(memory_space=pltpu.VMEM),) * 3,
        scratch_shapes=[pltpu.VMEM(v.shape, v.dtype) for v in operands[:5]] + [dma((8,))],
        compiler_params=pltpu.CompilerParams(vmem_limit_bytes=VMEM_LIMIT),
    )(*[pltpu.with_memory_space_constraint(v, pltpu.HBM) for v in operands])
    me = lax.axis_index("expert")

    def rows_for(c):
        if flight == 1:
            return own_rows[0]
        return lax.dynamic_index_in_dim(own_rows, (me ^ c) // SPLIT, 0, keepdims=False)

    arrived = [rows_for(0)]
    for c in range(1, chunks):
        if c % SPLIT == 3:
            arrived.append(swap(arrived[c - 1], "expert", 1))
        else:
            arrived.append(swap(rows_for(c), "expert", c))
    pairs = [(1, 2)] + [(i, i + 1) for i in range(4, chips, 2)]
    shards = [swap(own_weights, "dp", 2 * i) for i in reversed(range(1, chips))]
    half = call(
        join_kernel,
        struct((chips, 3 * hidden, width), jnp.bfloat16),
        [v[None] for v in (own_weights, *shards[::-1])],
        after=arrived[1:],
    )
    other_half = swap(half, "dp", 1)
    rows_shape = (2, 2, rows, width)
    own_block, single_block, *packed = call(
        functools.partial(repack_kernel, chunks, pairs),
        [struct(rows_shape, jnp.bfloat16)] * (2 + 2 * len(pairs)),
        arrived,
    )
    block_rows = [own_block, swap(single_block, "dp", 2 * SINGLE)]
    for n, pair in enumerate(pairs):
        mine, other = packed[2 * n : 2 * n + 2]
        both = call(
            join_rows_kernel,
            struct((2, 2, 2 * rows, width), jnp.bfloat16),
            (mine, swap(other, "dp", 1)),
        )
        block_rows.append(cross(both, pair))

    grads, near_parts, direct, relay = call(
        functools.partial(expert_kernel, chunks),
        [struct((rows, 3 * hidden), jnp.bfloat16)]
        + [struct((n * flight, blocks, CAP, width), jnp.bfloat16) for n in (2, 1, 1)],
        (*arrived, half, other_half),
        flops=5 * 10**9,
    )
    chip_grads = call(
        join_kernel,
        struct((2 * rows, 3 * hidden), jnp.bfloat16),
        (grads, swap(grads, "dp", 1)),
    )
    all_grads = [grads, swap(grads, "dp", 2 * SINGLE)]
    all_grads += [cross(chip_grads, pair) for pair in pairs]
    part = struct((flight, blocks, CAP, width), jnp.bfloat16)
    half_sum, direct = call(
        add_kernel,
        (part, part),
        (near_parts, swap(relay, "expert", 1), direct),
        after=block_rows[1:],
        flops=3 * 10**9,
    )
    pair_sum, direct = swap(half_sum, "expert", 2), swap(direct, "expert", 1)
    returned = (near_parts, pair_sum, direct)
    if flight > 1:
        slot_grad = call(sum_kernel, part, returned)
        returned = [slot_grad[0]]
        returned += [swap(slot_grad[j], "expert", SPLIT * j) for j in range(1, flight)]

    terms = (*block_rows, *all_grads)
    other_sum = call(
        functools.partial(weight_grad_kernel, 1),
        struct((3 * hidden, width), jnp.bfloat16),
        terms,
        after=(half_sum,),
        flops=10**10,
    )
    own_sum = call(
        functools.partial(weight_grad_kernel, 0),
        struct((3 * hidden, width), jnp.float32),
        terms,
        after=(other_sum,),
        flops=10**10,
    )
    other_sum = swap(other_sum, "dp", 1)
    grad_tokens, grad_gate, grad_up, grad_down = pl.pallas_call(
        functools.partial(finish_kernel, len(returned)),
        out_shape=[struct((count, model_width), jnp.bfloat16)]
        + [struct((hidden, width), jnp.float32)] * 3,
        in_specs=[pl.BlockSpec(memory_space=pltpu.VMEM)] * (3 + len(returned)),
        out_specs=[pl.BlockSpec(memory_space=pltpu.HBM)] * 4,
        scratch_shapes=[
            pltpu.VMEM((count, model_width), jnp.bfloat16),
            pltpu.VMEM((3 * hidden, width), jnp.float32),
            dma((7,)),
        ],
        compiler_params=pltpu.CompilerParams(vmem_limit_bytes=VMEM_LIMIT),
    )(own_sum, other_sum, hot, *returned)
    return grad_tokens, grad_gate.T, grad_up.T, grad_down


def solution(mesh):
    split_rows = P(("dp", "expert"), None)
    return jax.shard_map(
        body,
        mesh=mesh,
        in_specs=(split_rows,) * 5 + (P("dp", "expert"), P("dp", "expert"), P("expert", "dp")),
        out_specs=(split_rows, P("dp", "expert"), P("dp", "expert"), P("expert", "dp")),
        check_vma=False,
    )
```

```python
import functools

import jax
import jax.numpy as jnp
from jax import lax
from jax.experimental import pallas as pl
from jax.experimental.pallas import tpu as pltpu
from jax.sharding import PartitionSpec as P

SPLIT = 4
CAP = 16
SINGLE = 3
VMEM_LIMIT = 48 * 1024 * 1024

CONTRACT_LAST = (((1,), (1,)), ((), ()))
CONTRACT_FIRST = (((0,), (0,)), ((), ()))
PLAIN = (((1,), (0,)), ((), ()))


def dot(left, right, dims):
    return lax.dot_general(left, right, dims, preferred_element_type=jnp.float32)


def call(kernel, out_shape, args, after=(), flops=0):
    def run(*refs):
        kernel(*refs[: len(args)], *refs[len(args) + len(after) :])

    return pl.pallas_call(
        run,
        out_shape=out_shape,
        in_specs=[pl.BlockSpec(memory_space=pltpu.VMEM)] * len(args)
        + [pl.BlockSpec(memory_space=pl.ANY)] * len(after),
        out_specs=jax.tree.map(lambda _: pl.BlockSpec(memory_space=pltpu.VMEM), out_shape),
        compiler_params=pltpu.CompilerParams(vmem_limit_bytes=VMEM_LIMIT),
        cost_estimate=pl.CostEstimate(flops=flops, bytes_accessed=0, transcendentals=0),
    )(*args, *after)


def swap(values, axis, shift):
    size = lax.axis_size(axis)
    return lax.ppermute(values, axis, [(i, i ^ shift) for i in range(size)])


def cross(values, pair):
    size = lax.axis_size("dp")
    return lax.ppermute(values, "dp", [(i, i ^ (2 * pair[i % 2])) for i in range(size)])


def cross_cores(values, pair):
    size = lax.axis_size("dp")
    return lax.ppermute(values, "dp", [(i, i ^ (2 * pair[1 - i % 2] + 1)) for i in range(size)])


def begin_kernel(
    ids_hbm, mask_hbm, gate_hbm, tok_hbm, cot_hbm, gate_w_hbm, up_w_hbm, down_w_hbm,
    rows_ref, hot_ref, stack_ref,
    ids_ref, mask_ref, gate_ref, tok_ref, cot_ref, sems,
):
    flight, _, blocks, cap, width = rows_ref.shape
    hidden = gate_w_hbm.shape[0]
    pairs = [
        (ids_hbm, ids_ref),
        (mask_hbm, mask_ref),
        (gate_hbm, gate_ref),
        (tok_hbm, tok_ref),
        (cot_hbm, cot_ref),
        (gate_w_hbm, stack_ref.at[pl.ds(0, hidden)]),
        (up_w_hbm, stack_ref.at[pl.ds(hidden, hidden)]),
        (down_w_hbm, stack_ref.at[pl.ds(2 * hidden, hidden)]),
    ]
    copies = [
        pltpu.make_async_copy(source, target, sems.at[i])
        for i, (source, target) in enumerate(pairs)
    ]
    for copy in copies:
        copy.start()
    count = ids_ref.shape[1]
    earlier = (
        lax.broadcasted_iota(jnp.int32, (count, count), 0)
        < lax.broadcasted_iota(jnp.int32, (count, count), 1)
    ).astype(jnp.bfloat16)
    slot = lax.broadcasted_iota(jnp.int32, (cap, count), 0).astype(jnp.float32)
    for copy in copies[:3]:
        copy.wait()
    live = mask_ref[...] == 1
    gates = []
    for j in range(flight):
        hit = jnp.where((ids_ref[...] == j) & live, 1.0, 0.0)
        held = jnp.sum(hit, axis=0, keepdims=True)
        rank = jnp.sum(dot(hit.astype(jnp.bfloat16), earlier, PLAIN), axis=0, keepdims=True)
        gate = jnp.sum(hit * gate_ref[...], axis=0, keepdims=True)
        hot = jnp.where((slot == rank) & (held > 0.0), 1.0, 0.0)
        gates.append(jnp.sum(hot * gate, axis=1, keepdims=True))
        hot_ref[j] = hot.astype(jnp.bfloat16)
    for copy in copies[3:5]:
        copy.wait()
    for j in range(flight):
        picked = dot(hot_ref[j], tok_ref[...], PLAIN).astype(jnp.bfloat16)
        graded = (gates[j] * dot(hot_ref[j], cot_ref[...], PLAIN)).astype(jnp.bfloat16)
        for b in range(blocks):
            rows_ref[j, 0, b] = picked[:, b * width : (b + 1) * width]
            rows_ref[j, 1, b] = graded[:, b * width : (b + 1) * width]
    for copy in copies[5:]:
        copy.wait()


def join_kernel(*refs):
    out_ref, low = refs[-1], 0
    for ref in refs[:-1]:
        out_ref[low : low + ref.shape[0]] = ref[...]
        low += ref.shape[0]


def rows_of(row_refs, kind, block):
    return jnp.concatenate([r[kind, block] for r in row_refs], axis=0)


def own_shift(me, pair):
    first = lax.rem(me, 2) == 0
    return [2 * jnp.where(first, pair[i], pair[1 - i]) for i in range(2)]


def repack_kernel(chunks, pairs, *refs):
    me = lax.axis_index("dp")
    shifts = [0, 2 * SINGLE]
    for pair in pairs:
        mine, other = own_shift(me, pair)
        shifts += [mine, other ^ 1]
    for shift, out_ref in zip(shifts, refs[chunks:]):
        for kind in range(2):
            for k in range(2):
                out_ref[kind, k] = rows_of(refs[:chunks], kind, me ^ shift ^ k)


def expert_kernel(chunks, *refs):
    row_refs, (half_ref, other_ref, grads_ref) = refs[:chunks], refs[chunks : chunks + 3]
    near_part_ref, far_part_ref = refs[chunks + 3 :]
    flight = chunks // SPLIT
    me = lax.axis_index("dp")
    weights = []
    for i in range(half_ref.shape[0]):
        weights += [(half_ref.at[i], me ^ (2 * i)), (other_ref.at[i], me ^ (2 * i + 1))]
    hidden = half_ref.shape[1] // 3
    pre_gate, pre_up, grad_act = 0.0, 0.0, 0.0
    for weight_ref, block in weights:
        rows_in = rows_of(row_refs, 0, block)
        pre_gate += dot(rows_in, weight_ref[:hidden], CONTRACT_LAST)
        pre_up += dot(rows_in, weight_ref[hidden : 2 * hidden], CONTRACT_LAST)
        grad_act += dot(rows_of(row_refs, 1, block), weight_ref[2 * hidden :], CONTRACT_LAST)
    sigmoid_value = lax.logistic(pre_gate)
    silu_value = pre_gate * sigmoid_value
    slope = sigmoid_value * (1.0 + pre_gate * (1.0 - sigmoid_value))
    grad_gate_pre = (grad_act * pre_up * slope).astype(jnp.bfloat16)
    grad_up_pre = (grad_act * silu_value).astype(jnp.bfloat16)
    activated = (silu_value * pre_up).astype(jnp.bfloat16)
    grads_ref[...] = jnp.concatenate([grad_gate_pre, grad_up_pre, activated], axis=1)
    for weight_ref, block in weights:
        part = dot(grad_gate_pre, weight_ref[:hidden], PLAIN)
        part += dot(grad_up_pre, weight_ref[hidden : 2 * hidden], PLAIN)
        part = part.astype(jnp.bfloat16)
        for j in range(flight):
            for c, (part_ref, n) in enumerate(
                ((near_part_ref, j), (far_part_ref, j), (far_part_ref, flight + j), (near_part_ref, flight + j))
            ):
                low = (SPLIT * j + c) * CAP
                part_ref[n, block] = part[low : low + CAP]


def weight_grad_kernel(chips, sibling, *refs):
    out_ref, row_refs, grad_refs = refs[-1], refs[:chips], refs[chips:-1]
    hidden = out_ref.shape[0] // 3
    grads = jnp.concatenate([g[...] for g in grad_refs], axis=0)
    rows_in = jnp.concatenate([r[0, sibling] for r in row_refs], axis=0)
    rows_grad = jnp.concatenate([r[1, sibling] for r in row_refs], axis=0)
    pair = dot(grads[:, : 2 * hidden], rows_in, CONTRACT_FIRST)
    down = dot(grads[:, 2 * hidden :], rows_grad, CONTRACT_FIRST)
    out_ref[: 2 * hidden] = pair.astype(out_ref.dtype)
    out_ref[2 * hidden :] = down.astype(out_ref.dtype)


def add_kernel(near_ref, far_ref, out_ref):
    half = out_ref.shape[0]
    total = near_ref[half:].astype(jnp.float32) + far_ref[half:].astype(jnp.float32)
    out_ref[...] = total.astype(out_ref.dtype)


def sum_kernel(near_ref, far_ref, pair_ref, out_ref):
    half = out_ref.shape[0]
    total = near_ref[:half].astype(jnp.float32) + far_ref[:half].astype(jnp.float32)
    out_ref[...] = (total + pair_ref[...].astype(jnp.float32)).astype(out_ref.dtype)


def finish_kernel(chunks, own_ref, other_ref, hot_ref, *refs):
    part_refs, refs = refs[:chunks], refs[chunks:]
    out_hbm, *grad_hbm = refs[:4]
    out_ref, grad_ref, sems = refs[4:]
    hidden = grad_hbm[0].shape[0]
    copies = []

    def send(source, target):
        copies.append(pltpu.make_async_copy(source, target, sems.at[len(copies)]))
        copies[-1].start()

    for i, hbm in enumerate(grad_hbm):
        part = pl.ds(i * hidden, hidden)
        grad_ref[part] = own_ref[part] + other_ref[part].astype(jnp.float32)
        send(grad_ref.at[part], hbm)
    flight = hot_ref.shape[0]
    blocks, _, width = part_refs[0].shape[-3:]
    step = blocks * width // 4
    home = lax.axis_index("expert") // SPLIT
    for b in range(blocks):
        total = 0.0
        for j in range(flight):
            if flight == 1:
                near_ref, far_ref, pair_ref = part_refs
                summed = near_ref[0, b].astype(jnp.float32) + far_ref[0, b].astype(jnp.float32)
                summed = (summed + pair_ref[0, b].astype(jnp.float32)).astype(jnp.bfloat16)
            else:
                summed = part_refs[j][b]
            total += dot(hot_ref[home ^ j], summed, CONTRACT_FIRST)
        out_ref[:, b * width : (b + 1) * width] = total.astype(out_ref.dtype)
        if (b + 1) * width % step == 0:
            columns = pl.ds((b + 1) * width - step, step)
            send(out_ref.at[:, columns], out_hbm.at[:, columns])
    for copy in copies:
        copy.wait()


def body(tokens, cotangent, expert_ids, drop_mask, gate_table, gate_weight, up_weight, down_weight):
    chunks = lax.axis_size("expert")
    blocks = lax.axis_size("dp")
    flight = chunks // SPLIT
    count, model_width = tokens.shape
    width = model_width // blocks
    hidden = gate_weight.shape[1]
    rows = chunks * CAP
    struct = jax.ShapeDtypeStruct

    chips = blocks // 2
    dma = pltpu.SemaphoreType.DMA
    operands = (
        expert_ids.T, drop_mask.T, gate_table.T, tokens, cotangent,
        gate_weight.T, up_weight.T, down_weight,
    )
    own_rows, hot, own_weights = pl.pallas_call(
        begin_kernel,
        out_shape=(
            struct((flight, 2, blocks, CAP, width), jnp.bfloat16),
            struct((flight, CAP, count), jnp.bfloat16),
            struct((3 * hidden, width), jnp.bfloat16),
        ),
        in_specs=[pl.BlockSpec(memory_space=pltpu.HBM)] * 8,
        out_specs=(pl.BlockSpec(memory_space=pltpu.VMEM),) * 3,
        scratch_shapes=[pltpu.VMEM(v.shape, v.dtype) for v in operands[:5]] + [dma((8,))],
        compiler_params=pltpu.CompilerParams(vmem_limit_bytes=VMEM_LIMIT),
    )(*[pltpu.with_memory_space_constraint(v, pltpu.HBM) for v in operands])
    me = lax.axis_index("expert")

    def rows_for(c):
        if flight == 1:
            return own_rows[0]
        return lax.dynamic_index_in_dim(own_rows, (me ^ c) // SPLIT, 0, keepdims=False)

    arrived = [rows_for(0)] + [None] * (chunks - 1)
    for c in sorted(range(1, chunks), key=lambda c: c % SPLIT == 2):
        if c % SPLIT == 2:
            arrived[c] = swap(arrived[c + 1], "expert", 1)
        else:
            arrived[c] = swap(rows_for(c), "expert", c)
    pairs = [(1, 2)] + [(i, i + 1) for i in range(4, chips, 2)]
    shards = [swap(own_weights, "dp", 2 * i) for i in reversed(range(1, chips))]
    half = call(
        join_kernel,
        struct((chips, 3 * hidden, width), jnp.bfloat16),
        [v[None] for v in (own_weights, *shards[::-1])],
        after=arrived[1:],
    )
    other_half = swap(half, "dp", 1)
    rows_shape = (2, 2, rows, width)
    own_block, single_block, *packed = call(
        functools.partial(repack_kernel, chunks, pairs),
        [struct(rows_shape, jnp.bfloat16)] * (2 + 2 * len(pairs)),
        arrived,
    )
    block_rows = [own_block, swap(single_block, "dp", 2 * SINGLE)]
    for n, pair in enumerate(pairs):
        block_rows.append(cross(packed[2 * n], pair))
        block_rows.append(cross_cores(packed[2 * n + 1], pair))

    grads, near_parts, far_parts = call(
        functools.partial(expert_kernel, chunks),
        [struct((rows, 3 * hidden), jnp.bfloat16)]
        + [struct((2 * flight, blocks, CAP, width), jnp.bfloat16)] * 2,
        (*arrived, half, other_half),
        flops=5 * 10**9,
    )
    chip_grads = call(
        join_kernel,
        struct((2 * rows, 3 * hidden), jnp.bfloat16),
        (grads, swap(grads, "dp", 1)),
    )
    all_grads = [grads, swap(grads, "dp", 2 * SINGLE)]
    all_grads += [cross(chip_grads, pair) for pair in pairs]
    far_parts = swap(far_parts, "expert", 1)
    pair = struct((flight, blocks, CAP, width), jnp.bfloat16)
    pair_sum = call(add_kernel, pair, (near_parts, far_parts), after=block_rows[1:], flops=3 * 10**9)
    half_sum, pair_sum = pair_sum, swap(pair_sum, "expert", 3)
    returned = (near_parts, far_parts, pair_sum)
    if flight > 1:
        slot_grad = call(sum_kernel, pair, returned)
        returned = [slot_grad[0]]
        returned += [swap(slot_grad[j], "expert", SPLIT * j) for j in range(1, flight)]

    terms = (*block_rows, *all_grads)
    other_sum = call(
        functools.partial(weight_grad_kernel, chips, 1),
        struct((3 * hidden, width), jnp.bfloat16),
        terms,
        after=(half_sum,),
        flops=10**10,
    )
    own_sum = call(
        functools.partial(weight_grad_kernel, chips, 0),
        struct((3 * hidden, width), jnp.float32),
        terms,
        after=(other_sum,),
        flops=10**10,
    )
    other_sum = swap(other_sum, "dp", 1)
    grad_tokens, grad_gate, grad_up, grad_down = pl.pallas_call(
        functools.partial(finish_kernel, len(returned)),
        out_shape=[struct((count, model_width), jnp.bfloat16)]
        + [struct((hidden, width), jnp.float32)] * 3,
        in_specs=[pl.BlockSpec(memory_space=pltpu.VMEM)] * (3 + len(returned)),
        out_specs=[pl.BlockSpec(memory_space=pltpu.HBM)] * 4,
        scratch_shapes=[
            pltpu.VMEM((count, model_width), jnp.bfloat16),
            pltpu.VMEM((3 * hidden, width), jnp.float32),
            dma((7,)),
        ],
        compiler_params=pltpu.CompilerParams(vmem_limit_bytes=VMEM_LIMIT),
    )(own_sum, other_sum, hot, *returned)
    return grad_tokens, grad_gate.T, grad_up.T, grad_down


def solution(mesh):
    split_rows = P(("dp", "expert"), None)
    return jax.shard_map(
        body,
        mesh=mesh,
        in_specs=(split_rows,) * 5 + (P("dp", "expert"), P("dp", "expert"), P("expert", "dp")),
        out_specs=(split_rows, P("dp", "expert"), P("dp", "expert"), P("expert", "dp")),
        check_vma=False,
    )
```

```python
import functools

import jax
import jax.numpy as jnp
from jax import lax
from jax.experimental import pallas as pl
from jax.experimental.pallas import tpu as pltpu
from jax.sharding import PartitionSpec as P

SPLIT = 4
CAP = 16
SINGLE = 3
VMEM_LIMIT = 48 * 1024 * 1024

CONTRACT_LAST = (((1,), (1,)), ((), ()))
CONTRACT_FIRST = (((0,), (0,)), ((), ()))
PLAIN = (((1,), (0,)), ((), ()))


def dot(left, right, dims):
    return lax.dot_general(left, right, dims, preferred_element_type=jnp.float32)


def call(kernel, out_shape, args, after=(), flops=0):
    def run(*refs):
        kernel(*refs[: len(args)], *refs[len(args) + len(after) :])

    return pl.pallas_call(
        run,
        out_shape=out_shape,
        in_specs=[pl.BlockSpec(memory_space=pltpu.VMEM)] * len(args)
        + [pl.BlockSpec(memory_space=pl.ANY)] * len(after),
        out_specs=jax.tree.map(lambda _: pl.BlockSpec(memory_space=pltpu.VMEM), out_shape),
        compiler_params=pltpu.CompilerParams(vmem_limit_bytes=VMEM_LIMIT),
        cost_estimate=pl.CostEstimate(flops=flops, bytes_accessed=0, transcendentals=0),
    )(*args, *after)


def swap(values, axis, shift):
    size = lax.axis_size(axis)
    return lax.ppermute(values, axis, [(i, i ^ shift) for i in range(size)])


def cross(values, pair):
    size = lax.axis_size("dp")
    return lax.ppermute(values, "dp", [(i, i ^ (2 * pair[i % 2])) for i in range(size)])


def cross_cores(values, pair):
    size = lax.axis_size("dp")
    return lax.ppermute(values, "dp", [(i, i ^ (2 * pair[1 - i % 2] + 1)) for i in range(size)])


def begin_kernel(
    ids_hbm, mask_hbm, gate_hbm, tok_hbm, cot_hbm, gate_w_hbm, up_w_hbm, down_w_hbm,
    rows_ref, hot_ref, stack_ref,
    ids_ref, mask_ref, gate_ref, tok_ref, cot_ref, sems,
):
    flight, _, blocks, cap, width = rows_ref.shape
    hidden = gate_w_hbm.shape[0]
    pairs = [
        (ids_hbm, ids_ref),
        (mask_hbm, mask_ref),
        (gate_hbm, gate_ref),
        (tok_hbm, tok_ref),
        (cot_hbm, cot_ref),
        (gate_w_hbm, stack_ref.at[pl.ds(0, hidden)]),
        (up_w_hbm, stack_ref.at[pl.ds(hidden, hidden)]),
        (down_w_hbm, stack_ref.at[pl.ds(2 * hidden, hidden)]),
    ]
    copies = [
        pltpu.make_async_copy(source, target, sems.at[i])
        for i, (source, target) in enumerate(pairs)
    ]
    for copy in copies:
        copy.start()
    count = ids_ref.shape[1]
    earlier = (
        lax.broadcasted_iota(jnp.int32, (count, count), 0)
        < lax.broadcasted_iota(jnp.int32, (count, count), 1)
    ).astype(jnp.bfloat16)
    slot = lax.broadcasted_iota(jnp.int32, (cap, count), 0).astype(jnp.float32)
    for copy in copies[:3]:
        copy.wait()
    live = mask_ref[...] == 1
    gates = []
    for j in range(flight):
        hit = jnp.where((ids_ref[...] == j) & live, 1.0, 0.0)
        held = jnp.sum(hit, axis=0, keepdims=True)
        rank = jnp.sum(dot(hit.astype(jnp.bfloat16), earlier, PLAIN), axis=0, keepdims=True)
        gate = jnp.sum(hit * gate_ref[...], axis=0, keepdims=True)
        hot = jnp.where((slot == rank) & (held > 0.0), 1.0, 0.0)
        gates.append(jnp.sum(hot * gate, axis=1, keepdims=True))
        hot_ref[j] = hot.astype(jnp.bfloat16)
    for copy in copies[3:5]:
        copy.wait()
    for j in range(flight):
        picked = dot(hot_ref[j], tok_ref[...], PLAIN).astype(jnp.bfloat16)
        graded = (gates[j] * dot(hot_ref[j], cot_ref[...], PLAIN)).astype(jnp.bfloat16)
        for b in range(blocks):
            rows_ref[j, 0, b] = picked[:, b * width : (b + 1) * width]
            rows_ref[j, 1, b] = graded[:, b * width : (b + 1) * width]
    for copy in copies[5:]:
        copy.wait()


def join_kernel(*refs):
    out_ref, low = refs[-1], 0
    for ref in refs[:-1]:
        out_ref[low : low + ref.shape[0]] = ref[...]
        low += ref.shape[0]


def rows_of(row_refs, kind, block):
    return jnp.concatenate([r[kind, block] for r in row_refs], axis=0)


def own_shift(me, pair):
    first = lax.rem(me, 2) == 0
    return [2 * jnp.where(first, pair[i], pair[1 - i]) for i in range(2)]


def repack_kernel(chunks, pairs, *refs):
    me = lax.axis_index("dp")
    shifts = [0, 2 * SINGLE]
    for pair in pairs:
        mine, other = own_shift(me, pair)
        shifts += [mine, other ^ 1]
    for shift, out_ref in zip(shifts, refs[chunks:]):
        for kind in range(2):
            for k in range(2):
                out_ref[kind, k] = rows_of(refs[:chunks], kind, me ^ shift ^ k)


def expert_kernel(chunks, *refs):
    row_refs, (half_ref, other_ref, grads_ref) = refs[:chunks], refs[chunks : chunks + 3]
    near_ref, direct_ref, relay_ref = refs[chunks + 3 :]
    flight = chunks // SPLIT
    me = lax.axis_index("dp")
    weights = []
    for i in range(half_ref.shape[0]):
        weights += [(half_ref.at[i], me ^ (2 * i)), (other_ref.at[i], me ^ (2 * i + 1))]
    hidden = half_ref.shape[1] // 3
    pre_gate, pre_up, grad_act = 0.0, 0.0, 0.0
    for weight_ref, block in weights:
        rows_in = rows_of(row_refs, 0, block)
        pre_gate += dot(rows_in, weight_ref[:hidden], CONTRACT_LAST)
        pre_up += dot(rows_in, weight_ref[hidden : 2 * hidden], CONTRACT_LAST)
        grad_act += dot(rows_of(row_refs, 1, block), weight_ref[2 * hidden :], CONTRACT_LAST)
    sigmoid_value = lax.logistic(pre_gate)
    silu_value = pre_gate * sigmoid_value
    slope = sigmoid_value * (1.0 + pre_gate * (1.0 - sigmoid_value))
    grad_gate_pre = (grad_act * pre_up * slope).astype(jnp.bfloat16)
    grad_up_pre = (grad_act * silu_value).astype(jnp.bfloat16)
    activated = (silu_value * pre_up).astype(jnp.bfloat16)
    grads_ref[...] = jnp.concatenate([grad_gate_pre, grad_up_pre, activated], axis=1)
    for weight_ref, block in weights:
        part = dot(grad_gate_pre, weight_ref[:hidden], PLAIN)
        part += dot(grad_up_pre, weight_ref[hidden : 2 * hidden], PLAIN)
        part = part.astype(jnp.bfloat16)
        for j in range(flight):
            targets = ((near_ref, j), (direct_ref, j), (relay_ref, j), (near_ref, flight + j))
            for c, (part_ref, n) in enumerate(targets):
                low = (SPLIT * j + c) * CAP
                part_ref[n, block] = part[low : low + CAP]


def weight_grad_kernel(chips, sibling, *refs):
    out_ref, row_refs, grad_refs = refs[-1], refs[:chips], refs[chips:-1]
    hidden = out_ref.shape[0] // 3
    grads = jnp.concatenate([g[...] for g in grad_refs], axis=0)
    rows_in = jnp.concatenate([r[0, sibling] for r in row_refs], axis=0)
    rows_grad = jnp.concatenate([r[1, sibling] for r in row_refs], axis=0)
    pair = dot(grads[:, : 2 * hidden], rows_in, CONTRACT_FIRST)
    down = dot(grads[:, 2 * hidden :], rows_grad, CONTRACT_FIRST)
    out_ref[: 2 * hidden] = pair.astype(out_ref.dtype)
    out_ref[2 * hidden :] = down.astype(out_ref.dtype)


def add_kernel(near_ref, relay_ref, direct_ref, out_ref, direct_out_ref):
    direct_out_ref[...] = direct_ref[...]
    half = out_ref.shape[0]
    total = near_ref[half:].astype(jnp.float32) + relay_ref[...].astype(jnp.float32)
    out_ref[...] = total.astype(out_ref.dtype)


def sum_kernel(near_ref, pair_ref, direct_ref, out_ref):
    half = out_ref.shape[0]
    total = near_ref[:half].astype(jnp.float32) + direct_ref[...].astype(jnp.float32)
    out_ref[...] = (total + pair_ref[...].astype(jnp.float32)).astype(out_ref.dtype)


def finish_kernel(chunks, own_ref, other_ref, hot_ref, *refs):
    part_refs, refs = refs[:chunks], refs[chunks:]
    out_hbm, *grad_hbm = refs[:4]
    out_ref, grad_ref, sems = refs[4:]
    hidden = grad_hbm[0].shape[0]
    copies = []

    def send(source, target):
        copies.append(pltpu.make_async_copy(source, target, sems.at[len(copies)]))
        copies[-1].start()

    for i, hbm in enumerate(grad_hbm):
        part = pl.ds(i * hidden, hidden)
        grad_ref[part] = own_ref[part] + other_ref[part].astype(jnp.float32)
        send(grad_ref.at[part], hbm)
    flight = hot_ref.shape[0]
    blocks, _, width = part_refs[0].shape[-3:]
    step = blocks * width // 4
    home = lax.axis_index("expert") // SPLIT
    for b in range(blocks):
        total = 0.0
        for j in range(flight):
            if flight == 1:
                near_ref, pair_ref, direct_ref = part_refs
                summed = near_ref[0, b].astype(jnp.float32) + direct_ref[0, b].astype(jnp.float32)
                summed = (summed + pair_ref[0, b].astype(jnp.float32)).astype(jnp.bfloat16)
            else:
                summed = part_refs[j][b]
            total += dot(hot_ref[home ^ j], summed, CONTRACT_FIRST)
        out_ref[:, b * width : (b + 1) * width] = total.astype(out_ref.dtype)
        if (b + 1) * width % step == 0:
            columns = pl.ds((b + 1) * width - step, step)
            send(out_ref.at[:, columns], out_hbm.at[:, columns])
    for copy in copies:
        copy.wait()


def body(tokens, cotangent, expert_ids, drop_mask, gate_table, gate_weight, up_weight, down_weight):
    chunks = lax.axis_size("expert")
    blocks = lax.axis_size("dp")
    flight = chunks // SPLIT
    count, model_width = tokens.shape
    width = model_width // blocks
    hidden = gate_weight.shape[1]
    rows = chunks * CAP
    struct = jax.ShapeDtypeStruct

    chips = blocks // 2
    dma = pltpu.SemaphoreType.DMA
    operands = (
        expert_ids.T, drop_mask.T, gate_table.T, tokens, cotangent,
        gate_weight.T, up_weight.T, down_weight,
    )
    own_rows, hot, own_weights = pl.pallas_call(
        begin_kernel,
        out_shape=(
            struct((flight, 2, blocks, CAP, width), jnp.bfloat16),
            struct((flight, CAP, count), jnp.bfloat16),
            struct((3 * hidden, width), jnp.bfloat16),
        ),
        in_specs=[pl.BlockSpec(memory_space=pltpu.HBM)] * 8,
        out_specs=(pl.BlockSpec(memory_space=pltpu.VMEM),) * 3,
        scratch_shapes=[pltpu.VMEM(v.shape, v.dtype) for v in operands[:5]] + [dma((8,))],
        compiler_params=pltpu.CompilerParams(vmem_limit_bytes=VMEM_LIMIT),
    )(*[pltpu.with_memory_space_constraint(v, pltpu.HBM) for v in operands])
    me = lax.axis_index("expert")

    def rows_for(c):
        if flight == 1:
            return own_rows[0]
        return lax.dynamic_index_in_dim(own_rows, (me ^ c) // SPLIT, 0, keepdims=False)

    arrived = [rows_for(0)] + [None] * (chunks - 1)
    for c in sorted(range(1, chunks), key=lambda c: c % SPLIT == 2):
        if c % SPLIT == 2:
            arrived[c] = swap(arrived[c + 1], "expert", 1)
        else:
            arrived[c] = swap(rows_for(c), "expert", c)
    pairs = [(1, 2)] + [(i, i + 1) for i in range(4, chips, 2)]
    shards = [swap(own_weights, "dp", 2 * i) for i in reversed(range(1, chips))]
    half = call(
        join_kernel,
        struct((chips, 3 * hidden, width), jnp.bfloat16),
        [v[None] for v in (own_weights, *shards[::-1])],
        after=arrived[1:],
    )
    other_half = swap(half, "dp", 1)
    rows_shape = (2, 2, rows, width)
    own_block, single_block, *packed = call(
        functools.partial(repack_kernel, chunks, pairs),
        [struct(rows_shape, jnp.bfloat16)] * (2 + 2 * len(pairs)),
        arrived,
    )
    block_rows = [own_block, swap(single_block, "dp", 2 * SINGLE)]
    for n, pair in enumerate(pairs):
        block_rows.append(cross(packed[2 * n], pair))
        block_rows.append(cross_cores(packed[2 * n + 1], pair))

    grads, near_parts, direct, relay = call(
        functools.partial(expert_kernel, chunks),
        [struct((rows, 3 * hidden), jnp.bfloat16)]
        + [struct((n * flight, blocks, CAP, width), jnp.bfloat16) for n in (2, 1, 1)],
        (*arrived, half, other_half),
        flops=5 * 10**9,
    )
    chip_grads = call(
        join_kernel,
        struct((2 * rows, 3 * hidden), jnp.bfloat16),
        (grads, swap(grads, "dp", 1)),
    )
    all_grads = [grads, swap(grads, "dp", 2 * SINGLE)]
    all_grads += [cross(chip_grads, pair) for pair in pairs]
    part = struct((flight, blocks, CAP, width), jnp.bfloat16)
    half_sum, direct = call(
        add_kernel,
        (part, part),
        (near_parts, swap(relay, "expert", 1), direct),
        after=block_rows[1:],
        flops=3 * 10**9,
    )
    pair_sum, direct = swap(half_sum, "expert", 3), swap(direct, "expert", 1)
    returned = (near_parts, pair_sum, direct)
    if flight > 1:
        slot_grad = call(sum_kernel, part, returned)
        returned = [slot_grad[0]]
        returned += [swap(slot_grad[j], "expert", SPLIT * j) for j in range(1, flight)]

    terms = (*block_rows, *all_grads)
    other_sum = call(
        functools.partial(weight_grad_kernel, chips, 1),
        struct((3 * hidden, width), jnp.bfloat16),
        terms,
        after=(half_sum,),
        flops=10**10,
    )
    own_sum = call(
        functools.partial(weight_grad_kernel, chips, 0),
        struct((3 * hidden, width), jnp.float32),
        terms,
        after=(other_sum,),
        flops=10**10,
    )
    other_sum = swap(other_sum, "dp", 1)
    grad_tokens, grad_gate, grad_up, grad_down = pl.pallas_call(
        functools.partial(finish_kernel, len(returned)),
        out_shape=[struct((count, model_width), jnp.bfloat16)]
        + [struct((hidden, width), jnp.float32)] * 3,
        in_specs=[pl.BlockSpec(memory_space=pltpu.VMEM)] * (3 + len(returned)),
        out_specs=[pl.BlockSpec(memory_space=pltpu.HBM)] * 4,
        scratch_shapes=[
            pltpu.VMEM((count, model_width), jnp.bfloat16),
            pltpu.VMEM((3 * hidden, width), jnp.float32),
            dma((7,)),
        ],
        compiler_params=pltpu.CompilerParams(vmem_limit_bytes=VMEM_LIMIT),
    )(own_sum, other_sum, hot, *returned)
    return grad_tokens, grad_gate.T, grad_up.T, grad_down


def solution(mesh):
    split_rows = P(("dp", "expert"), None)
    return jax.shard_map(
        body,
        mesh=mesh,
        in_specs=(split_rows,) * 5 + (P("dp", "expert"), P("dp", "expert"), P("expert", "dp")),
        out_specs=(split_rows, P("dp", "expert"), P("dp", "expert"), P("expert", "dp")),
        check_vma=False,
    )
```

```python
import functools

import jax
import jax.numpy as jnp
from jax import lax
from jax.experimental import pallas as pl
from jax.experimental.pallas import tpu as pltpu
from jax.sharding import PartitionSpec as P

SPLIT = 4
CAP = 16
SINGLE = 3
VMEM_LIMIT = 48 * 1024 * 1024

CONTRACT_LAST = (((1,), (1,)), ((), ()))
CONTRACT_FIRST = (((0,), (0,)), ((), ()))
PLAIN = (((1,), (0,)), ((), ()))


def dot(left, right, dims):
    return lax.dot_general(left, right, dims, preferred_element_type=jnp.float32)


def call(kernel, out_shape, args, after=(), flops=0):
    def run(*refs):
        kernel(*refs[: len(args)], *refs[len(args) + len(after) :])

    return pl.pallas_call(
        run,
        out_shape=out_shape,
        in_specs=[pl.BlockSpec(memory_space=pltpu.VMEM)] * len(args)
        + [pl.BlockSpec(memory_space=pl.ANY)] * len(after),
        out_specs=jax.tree.map(lambda _: pl.BlockSpec(memory_space=pltpu.VMEM), out_shape),
        compiler_params=pltpu.CompilerParams(vmem_limit_bytes=VMEM_LIMIT),
        cost_estimate=pl.CostEstimate(flops=flops, bytes_accessed=0, transcendentals=0),
    )(*args, *after)


def swap(values, axis, shift):
    size = lax.axis_size(axis)
    return lax.ppermute(values, axis, [(i, i ^ shift) for i in range(size)])


def cross(values, pair):
    size = lax.axis_size("dp")
    return lax.ppermute(values, "dp", [(i, i ^ (2 * pair[i % 2])) for i in range(size)])


def cross_cores(values, pair):
    size = lax.axis_size("dp")
    return lax.ppermute(values, "dp", [(i, i ^ (2 * pair[1 - i % 2] + 1)) for i in range(size)])


def begin_kernel(
    ids_hbm, mask_hbm, gate_hbm, tok_hbm, cot_hbm, gate_w_hbm, up_w_hbm, down_w_hbm,
    rows_ref, hot_ref, stack_ref,
    ids_ref, mask_ref, gate_ref, tok_ref, cot_ref, sems,
):
    flight, _, blocks, cap, width = rows_ref.shape
    hidden = gate_w_hbm.shape[0]
    pairs = [
        (ids_hbm, ids_ref),
        (mask_hbm, mask_ref),
        (gate_hbm, gate_ref),
        (tok_hbm, tok_ref),
        (cot_hbm, cot_ref),
        (gate_w_hbm, stack_ref.at[pl.ds(0, hidden)]),
        (up_w_hbm, stack_ref.at[pl.ds(hidden, hidden)]),
        (down_w_hbm, stack_ref.at[pl.ds(2 * hidden, hidden)]),
    ]
    copies = [
        pltpu.make_async_copy(source, target, sems.at[i])
        for i, (source, target) in enumerate(pairs)
    ]
    for copy in copies:
        copy.start()
    count = ids_ref.shape[1]
    earlier = (
        lax.broadcasted_iota(jnp.int32, (count, count), 0)
        < lax.broadcasted_iota(jnp.int32, (count, count), 1)
    ).astype(jnp.bfloat16)
    slot = lax.broadcasted_iota(jnp.int32, (cap, count), 0).astype(jnp.float32)
    for copy in copies[:3]:
        copy.wait()
    live = mask_ref[...] == 1
    gates = []
    for j in range(flight):
        hit = jnp.where((ids_ref[...] == j) & live, 1.0, 0.0)
        held = jnp.sum(hit, axis=0, keepdims=True)
        rank = jnp.sum(dot(hit.astype(jnp.bfloat16), earlier, PLAIN), axis=0, keepdims=True)
        gate = jnp.sum(hit * gate_ref[...], axis=0, keepdims=True)
        hot = jnp.where((slot == rank) & (held > 0.0), 1.0, 0.0)
        gates.append(jnp.sum(hot * gate, axis=1, keepdims=True))
        hot_ref[j] = hot.astype(jnp.bfloat16)
    for copy in copies[3:5]:
        copy.wait()
    for j in range(flight):
        picked = dot(hot_ref[j], tok_ref[...], PLAIN).astype(jnp.bfloat16)
        graded = (gates[j] * dot(hot_ref[j], cot_ref[...], PLAIN)).astype(jnp.bfloat16)
        for b in range(blocks):
            rows_ref[j, 0, b] = picked[:, b * width : (b + 1) * width]
            rows_ref[j, 1, b] = graded[:, b * width : (b + 1) * width]
    for copy in copies[5:]:
        copy.wait()


def join_kernel(*refs):
    out_ref, low = refs[-1], 0
    for ref in refs[:-1]:
        out_ref[low : low + ref.shape[0]] = ref[...]
        low += ref.shape[0]


def rows_of(row_refs, kind, block):
    return jnp.concatenate([r[kind, block] for r in row_refs], axis=0)


def own_shift(me, pair):
    first = lax.rem(me, 2) == 0
    return [2 * jnp.where(first, pair[i], pair[1 - i]) for i in range(2)]


def repack_kernel(chunks, pairs, *refs):
    me = lax.axis_index("dp")
    shifts = [0, 2 * SINGLE]
    for pair in pairs:
        mine, other = own_shift(me, pair)
        shifts += [mine, other ^ 1]
    for shift, out_ref in zip(shifts, refs[chunks:]):
        for kind in range(2):
            for k in range(2):
                out_ref[kind, k] = rows_of(refs[:chunks], kind, me ^ shift ^ k)


def expert_kernel(chunks, *refs):
    row_refs, (half_ref, other_ref, grads_ref) = refs[:chunks], refs[chunks : chunks + 3]
    near_ref, direct_ref, relay_ref = refs[chunks + 3 :]
    flight = chunks // SPLIT
    me = lax.axis_index("dp")
    weights = []
    for i in range(half_ref.shape[0]):
        weights += [(half_ref.at[i], me ^ (2 * i)), (other_ref.at[i], me ^ (2 * i + 1))]
    hidden = half_ref.shape[1] // 3
    pre_gate, pre_up, grad_act = 0.0, 0.0, 0.0
    for weight_ref, block in weights:
        rows_in = rows_of(row_refs, 0, block)
        pre_gate += dot(rows_in, weight_ref[:hidden], CONTRACT_LAST)
        pre_up += dot(rows_in, weight_ref[hidden : 2 * hidden], CONTRACT_LAST)
        grad_act += dot(rows_of(row_refs, 1, block), weight_ref[2 * hidden :], CONTRACT_LAST)
    sigmoid_value = lax.logistic(pre_gate)
    silu_value = pre_gate * sigmoid_value
    slope = sigmoid_value * (1.0 + pre_gate * (1.0 - sigmoid_value))
    grad_gate_pre = (grad_act * pre_up * slope).astype(jnp.bfloat16)
    grad_up_pre = (grad_act * silu_value).astype(jnp.bfloat16)
    activated = (silu_value * pre_up).astype(jnp.bfloat16)
    grads_ref[...] = jnp.concatenate([grad_gate_pre, grad_up_pre, activated], axis=1)
    for weight_ref, block in weights:
        part = dot(grad_gate_pre, weight_ref[:hidden], PLAIN)
        part += dot(grad_up_pre, weight_ref[hidden : 2 * hidden], PLAIN)
        part = part.astype(jnp.bfloat16)
        for j in range(flight):
            targets = ((near_ref, j), (direct_ref, j), (relay_ref, j), (near_ref, flight + j))
            for c, (part_ref, n) in enumerate(targets):
                low = (SPLIT * j + c) * CAP
                part_ref[n, block] = part[low : low + CAP]


def weight_grad_kernel(chips, sibling, *refs):
    out_ref, row_refs, grad_refs = refs[-1], refs[:chips], refs[chips:-1]
    hidden = out_ref.shape[0] // 3
    grads = jnp.concatenate([g[...] for g in grad_refs], axis=0)
    rows_in = jnp.concatenate([r[0, sibling] for r in row_refs], axis=0)
    rows_grad = jnp.concatenate([r[1, sibling] for r in row_refs], axis=0)
    pair = dot(grads[:, : 2 * hidden], rows_in, CONTRACT_FIRST)
    down = dot(grads[:, 2 * hidden :], rows_grad, CONTRACT_FIRST)
    out_ref[: 2 * hidden] = pair.astype(out_ref.dtype)
    out_ref[2 * hidden :] = down.astype(out_ref.dtype)


def add_kernel(near_ref, relay_ref, out_ref):
    half = out_ref.shape[0]
    total = near_ref[half:].astype(jnp.float32) + relay_ref[...].astype(jnp.float32)
    out_ref[...] = total.astype(out_ref.dtype)


def sum_kernel(near_ref, pair_ref, direct_ref, out_ref):
    half = out_ref.shape[0]
    total = near_ref[:half].astype(jnp.float32) + direct_ref[...].astype(jnp.float32)
    out_ref[...] = (total + pair_ref[...].astype(jnp.float32)).astype(out_ref.dtype)


def finish_kernel(chunks, own_ref, other_ref, hot_ref, *refs):
    part_refs, refs = refs[:chunks], refs[chunks:]
    out_hbm, *grad_hbm = refs[:4]
    out_ref, grad_ref, sems = refs[4:]
    hidden = grad_hbm[0].shape[0]
    copies = []

    def send(source, target):
        copies.append(pltpu.make_async_copy(source, target, sems.at[len(copies)]))
        copies[-1].start()

    for i, hbm in enumerate(grad_hbm):
        part = pl.ds(i * hidden, hidden)
        grad_ref[part] = own_ref[part] + other_ref[part].astype(jnp.float32)
        send(grad_ref.at[part], hbm)
    flight = hot_ref.shape[0]
    blocks, _, width = part_refs[0].shape[-3:]
    step = blocks * width // 4
    home = lax.axis_index("expert") // SPLIT
    for b in range(blocks):
        total = 0.0
        for j in range(flight):
            if flight == 1:
                near_ref, pair_ref, direct_ref = part_refs
                summed = near_ref[0, b].astype(jnp.float32) + direct_ref[0, b].astype(jnp.float32)
                summed = (summed + pair_ref[0, b].astype(jnp.float32)).astype(jnp.bfloat16)
            else:
                summed = part_refs[j][b]
            total += dot(hot_ref[home ^ j], summed, CONTRACT_FIRST)
        out_ref[:, b * width : (b + 1) * width] = total.astype(out_ref.dtype)
        if (b + 1) * width % step == 0:
            columns = pl.ds((b + 1) * width - step, step)
            send(out_ref.at[:, columns], out_hbm.at[:, columns])
    for copy in copies:
        copy.wait()


def body(tokens, cotangent, expert_ids, drop_mask, gate_table, gate_weight, up_weight, down_weight):
    chunks = lax.axis_size("expert")
    blocks = lax.axis_size("dp")
    flight = chunks // SPLIT
    count, model_width = tokens.shape
    width = model_width // blocks
    hidden = gate_weight.shape[1]
    rows = chunks * CAP
    struct = jax.ShapeDtypeStruct

    chips = blocks // 2
    dma = pltpu.SemaphoreType.DMA
    operands = (
        expert_ids.T, drop_mask.T, gate_table.T, tokens, cotangent,
        gate_weight.T, up_weight.T, down_weight,
    )
    own_rows, hot, own_weights = pl.pallas_call(
        begin_kernel,
        out_shape=(
            struct((flight, 2, blocks, CAP, width), jnp.bfloat16),
            struct((flight, CAP, count), jnp.bfloat16),
            struct((3 * hidden, width), jnp.bfloat16),
        ),
        in_specs=[pl.BlockSpec(memory_space=pltpu.HBM)] * 8,
        out_specs=(pl.BlockSpec(memory_space=pltpu.VMEM),) * 3,
        scratch_shapes=[pltpu.VMEM(v.shape, v.dtype) for v in operands[:5]] + [dma((8,))],
        compiler_params=pltpu.CompilerParams(vmem_limit_bytes=VMEM_LIMIT),
    )(*[pltpu.with_memory_space_constraint(v, pltpu.HBM) for v in operands])
    me = lax.axis_index("expert")

    def rows_for(c):
        if flight == 1:
            return own_rows[0]
        return lax.dynamic_index_in_dim(own_rows, (me ^ c) // SPLIT, 0, keepdims=False)

    arrived = [rows_for(0)] + [None] * (chunks - 1)
    for c in sorted(range(1, chunks), key=lambda c: c % SPLIT == 2):
        if c % SPLIT == 2:
            arrived[c] = swap(arrived[c + 1], "expert", 1)
        else:
            arrived[c] = swap(rows_for(c), "expert", c)
    pairs = [(1, 2)] + [(i, i + 1) for i in range(4, chips, 2)]
    shards = [swap(own_weights, "dp", 2 * i) for i in reversed(range(1, chips))]
    half = call(
        join_kernel,
        struct((chips, 3 * hidden, width), jnp.bfloat16),
        [v[None] for v in (own_weights, *shards[::-1])],
        after=arrived[1:],
    )
    other_half = swap(half, "dp", 1)
    rows_shape = (2, 2, rows, width)
    own_block, single_block, *packed = call(
        functools.partial(repack_kernel, chunks, pairs),
        [struct(rows_shape, jnp.bfloat16)] * (2 + 2 * len(pairs)),
        arrived,
    )
    block_rows = [own_block, swap(single_block, "dp", 2 * SINGLE)]
    for n, pair in enumerate(pairs):
        block_rows.append(cross(packed[2 * n], pair))
        block_rows.append(cross_cores(packed[2 * n + 1], pair))

    grads, near_parts, direct, relay = call(
        functools.partial(expert_kernel, chunks),
        [struct((rows, 3 * hidden), jnp.bfloat16)]
        + [struct((n * flight, blocks, CAP, width), jnp.bfloat16) for n in (2, 1, 1)],
        (*arrived, half, other_half),
        flops=5 * 10**9,
    )
    chip_grads = call(
        join_kernel,
        struct((2 * rows, 3 * hidden), jnp.bfloat16),
        (grads, swap(grads, "dp", 1)),
    )
    all_grads = [grads, swap(grads, "dp", 2 * SINGLE)]
    all_grads += [cross(chip_grads, pair) for pair in pairs]
    part = struct((flight, blocks, CAP, width), jnp.bfloat16)
    direct = swap(direct, "expert", 1)
    half_sum = call(
        add_kernel,
        part,
        (near_parts, swap(relay, "expert", 1)),
        after=block_rows[1:],
        flops=15 * 10**8,
    )
    pair_sum = swap(half_sum, "expert", 3)
    returned = (near_parts, pair_sum, direct)
    if flight > 1:
        slot_grad = call(sum_kernel, part, returned)
        returned = [slot_grad[0]]
        returned += [swap(slot_grad[j], "expert", SPLIT * j) for j in range(1, flight)]

    terms = (*block_rows, *all_grads)
    other_sum = call(
        functools.partial(weight_grad_kernel, chips, 1),
        struct((3 * hidden, width), jnp.bfloat16),
        terms,
        after=(half_sum,),
        flops=10**10,
    )
    own_sum = call(
        functools.partial(weight_grad_kernel, chips, 0),
        struct((3 * hidden, width), jnp.float32),
        terms,
        after=(other_sum,),
        flops=10**10,
    )
    other_sum = swap(other_sum, "dp", 1)
    grad_tokens, grad_gate, grad_up, grad_down = pl.pallas_call(
        functools.partial(finish_kernel, len(returned)),
        out_shape=[struct((count, model_width), jnp.bfloat16)]
        + [struct((hidden, width), jnp.float32)] * 3,
        in_specs=[pl.BlockSpec(memory_space=pltpu.VMEM)] * (3 + len(returned)),
        out_specs=[pl.BlockSpec(memory_space=pltpu.HBM)] * 4,
        scratch_shapes=[
            pltpu.VMEM((count, model_width), jnp.bfloat16),
            pltpu.VMEM((3 * hidden, width), jnp.float32),
            dma((7,)),
        ],
        compiler_params=pltpu.CompilerParams(vmem_limit_bytes=VMEM_LIMIT),
    )(own_sum, other_sum, hot, *returned)
    return grad_tokens, grad_gate.T, grad_up.T, grad_down


def solution(mesh):
    split_rows = P(("dp", "expert"), None)
    return jax.shard_map(
        body,
        mesh=mesh,
        in_specs=(split_rows,) * 5 + (P("dp", "expert"), P("dp", "expert"), P("expert", "dp")),
        out_specs=(split_rows, P("dp", "expert"), P("dp", "expert"), P("expert", "dp")),
        check_vma=False,
    )
```
